512 devices in a mesh: gx: 32 (over y, z_lo, core), gy: 16 (over x, z_hi).
Axes of the slice: x: 4, y: 8, z: 8 (z_hi: 4, z_lo: 2; z = z_hi * 2 + z_lo), core: 2. Of those that a mesh axis runs over, the one named last changes fastest.
Arguments:
- field: bfloat16 [512, 256, 4, 64], P('gx', 'gy'), may hold values from -6 to 6
- first_kernel: bfloat16 [1728, 64], replicated, may hold values from -0.21875 to 0.21875
- second_kernel: bfloat16 [1728, 64], replicated, may hold values from -0.15625 to 0.15625
- cotangent: bfloat16 [512, 256, 4, 64], P('gx', 'gy'), may hold values from -6 to 6
- samples: int32 [32, 16, 256], P('gx', 'gy'), may hold values from 0 to 1023
Outputs:
- output: bfloat16 [512, 256, 4, 64], P('gx', 'gy')
- first_update: float32 [1728, 64], replicated
- second_update: float32 [1728, 64], replicated
The draws below stay inside these ranges and needn't reach their ends.
All inputs are finite; a program needn't handle non-finite values.
Results may differ from the reference program's by a relative error of at most 0.0034.
Values may be sent and summed in bfloat16 or wider, within the bound.
A program may use at most 64 MiB of HBM per device.

```python
import jax
import jax.numpy as jnp
from jax import lax

C = 64
TAPS = 27
TX = 16
TY = 16
NZ = 4
SAMP = 256
NS_ITERS = 5
NX = 512
NY = 256
N_GX = 32
N_GY = 16


def place_ends(drawn, key, least, top_value):
    shape = drawn.shape
    place = [jax.random.randint(jax.random.fold_in(key, axis), (), 0, shape[axis]) for axis in range(len(shape))]
    drawn = drawn.at[tuple(place)].set(least)
    longest = shape.index(max(shape))
    place[longest] = (place[longest] + 1) % shape[longest]
    return drawn.at[tuple(place)].set(top_value)


def shard_levels(own_key, shape, shards, low, largest):
    def one(axis_at, parts):
        draws = jax.random.uniform(jax.random.fold_in(jax.random.fold_in(own_key, 6), axis_at), (parts,), jnp.float32, low / len(shards), largest / len(shards))
        return jnp.repeat(jnp.exp(draws), shape[axis_at] // parts).reshape((-1,) + (1,) * (len(shape) - axis_at - 1))

    level = one(*shards[0])
    for cut in shards[1:]:
        level = level * one(*cut)
    return level


def scatter_about(rng, extent, deviation, limit, cuts=(), held_as=jnp.bfloat16):
    drawn = deviation * jax.random.normal(rng, extent, jnp.float32)
    if cuts:
        drawn = drawn * shard_levels(rng, extent, cuts, -0.22, 0.18)
    return jnp.clip(drawn, -limit, limit).astype(held_as)


def setup_inputs(seed: int = 0) -> dict:
    streams_of = jax.random.split(jax.random.key(seed), 6)
    return {
        "field": scatter_about(streams_of[0], (NX, NY, NZ, C), 1.0, 6.0, ((0, 32), (1, 16))),
        "first_kernel": scatter_about(streams_of[1], (TAPS * C, C), (TAPS * C // 2) ** -0.5, 0.21875),
        "second_kernel": scatter_about(streams_of[2], (TAPS * C, C), (TAPS * C) ** -0.5, 0.15625),
        "cotangent": scatter_about(streams_of[3], (NX, NY, NZ, C), 1.0, 6.0, ((0, 32), (1, 16))),
        "samples": place_ends(jax.random.randint(streams_of[4], (N_GX, N_GY, SAMP), 0, TX * TY * NZ), jax.random.fold_in(streams_of[4], 1), 0, (TX * TY * NZ) - 1).astype(jnp.int32),
    }


def patches(padded, row_index, ylen, zlen):
    slab = lax.dynamic_slice_in_dim(padded, row_index, 3, 0)
    pieces = [slab[first, second:second + ylen, third:third + zlen, :] for first in range(3) for second in range(3) for third in range(3)]
    return jnp.concatenate(pieces, -1).reshape(ylen * zlen, -1)

def convolve(framed, kernel):
    padded = jnp.pad(framed, ((0, 0), (0, 0), (1, 1), (0, 0)))
    xlen = framed.shape[0] - 2
    ylen = framed.shape[1] - 2
    zlen = framed.shape[2]
    width = kernel.shape[1]

    def one_row(row_index):
        return jnp.dot(patches(padded, row_index, ylen, zlen), kernel, preferred_element_type=jnp.float32)
    result = lax.map(one_row, jnp.arange(xlen, dtype=jnp.int32))
    return result.reshape(xlen, ylen, zlen, width)

def kernel_grad(framed, grads):
    padded = jnp.pad(framed, ((0, 0), (0, 0), (1, 1), (0, 0)))
    xlen, ylen, zlen, width = grads.shape

    def add_row(row_index, total):
        block = lax.dynamic_index_in_dim(grads, row_index, 0, keepdims=False).reshape(ylen * zlen, width)
        return total + jnp.dot(patches(padded, row_index, ylen, zlen).T, block, preferred_element_type=jnp.float32)
    start = jnp.zeros((27 * framed.shape[3], width), jnp.float32)
    return lax.fori_loop(0, xlen, add_row, start)

def flip_kernel(kernel, width):
    blocks = kernel.reshape(3, 3, 3, width, width)[::-1, ::-1, ::-1]
    return jnp.transpose(blocks, (0, 1, 2, 4, 3)).reshape(27 * width, width)

def newton_inverse(factor):
    width = factor.shape[0]
    identity = jnp.eye(width, dtype=jnp.float32)
    matrix = factor + 0.1 * identity
    approx = identity / jnp.sqrt(jnp.sum(matrix * matrix))
    for step in range(NS_ITERS):
        inner = 2.0 * identity - jnp.dot(matrix, approx, precision=lax.Precision.HIGHEST)
        approx = jnp.dot(approx, inner, precision=lax.Precision.HIGHEST)
    return approx

def precondition(grad, left_inv, right_inv, width):
    blocks = grad.reshape(27, width, width)
    result = jnp.einsum('ab,tbc,cd->tad', left_inv, blocks, right_inv, precision=lax.Precision.HIGHEST)
    return result.reshape(27 * width, width)

def sampled_gram(values, samples):
    width = values.shape[3]
    tiles = values.reshape(N_GX, TX, N_GY, TY, NZ, width).transpose(0, 2, 1, 3, 4, 5).reshape(N_GX, N_GY, TX * TY * NZ, width)
    picked = jnp.take_along_axis(tiles, samples.astype(jnp.int32)[..., None], axis=2).reshape(-1, width)
    gram = jnp.dot(picked.T, picked, preferred_element_type=jnp.float32)
    return gram / (N_GX * N_GY * SAMP)

def reference(field, first_kernel, second_kernel, cotangent, samples):
    width = field.shape[3]
    frame = ((1, 1), (1, 1), (0, 0), (0, 0))
    framed_field = jnp.pad(field, frame)
    hidden_pre = convolve(framed_field, first_kernel)
    hidden = jax.nn.silu(hidden_pre).astype(jnp.bfloat16)
    framed_hidden = jnp.pad(hidden, frame)
    output = (field.astype(jnp.float32) + convolve(framed_hidden, second_kernel)).astype(jnp.bfloat16)
    back = convolve(jnp.pad(cotangent, frame), flip_kernel(second_kernel, width))
    sigma = jax.nn.sigmoid(hidden_pre)
    delta = (back * sigma * (1.0 + hidden_pre * (1.0 - sigma))).astype(jnp.bfloat16)
    scale = 1.0 / jnp.sqrt(jnp.float32(NX * NY * NZ))
    second_grad = kernel_grad(framed_hidden, cotangent) * scale
    first_grad = kernel_grad(framed_field, delta) * scale
    second_update = precondition(second_grad, newton_inverse(sampled_gram(hidden, samples)), newton_inverse(sampled_gram(cotangent, samples)), width)
    first_update = precondition(first_grad, newton_inverse(sampled_gram(field, samples)), newton_inverse(sampled_gram(delta, samples)), width)
    return (output, first_update, second_update)
```

```python
import functools

import jax
import jax.numpy as jnp
from jax import lax
from jax.experimental import pallas as pl
from jax.experimental.pallas import tpu as pltpu
from jax.sharding import PartitionSpec as P

MESH = pl.DeviceIdType.MESH
F32 = jnp.float32
BF16 = jnp.bfloat16
NS_ITERS = 5
C = 64
TX = 16
TY = 16
NZ = 4
WIDE = NZ * C
CELLS = TX * TY
BLOCKS = 32
HALF = BLOCKS * 64 // 2
FIELD, COT, HIDDEN = 0, 1, 2
NN = (((1,), (0,)), ((), ()))
NT = (((1,), (1,)), ((), ()))


def dot(a, b, dims=NN):
    return lax.dot_general(a, b, dims, preferred_element_type=F32)


def dot32(a, b, dims=NN):
    return lax.dot_general(a, b, dims, precision=lax.Precision.HIGHEST, preferred_element_type=F32)


def iota(shape, dim):
    return lax.broadcasted_iota(jnp.int32, shape, dim)


def onehot(target, shape):
    return jnp.where(iota(shape, 1) == target, 1.0, 0.0).astype(BF16)


def swap_halves(value):
    return pltpu.roll(value, 64, 1)


def kernel(
    sizes,
    field_ref,
    first_ref,
    second_ref,
    cot_ref,
    samples_ref,
    out_ref,
    first_out,
    second_out,
    src,
    col,
    cat,
    band,
    grads,
    pay,
    core_in,
    axis_in,
    plane_out,
    plane_in,
    full,
    metric,
    halo_send,
    halo_recv,
    core_send,
    core_recv,
    axis_send,
    axis_recv,
    plane_send,
    plane_recv,
    gather_send,
    gather_recv,
    spread_send,
    spread_recv,
    back_send,
    back_recv,
):
    n_gx, n_gy, z_hi, ring, plane, part = sizes
    gx = lax.axis_index("gx")
    gy = lax.axis_index("gy")
    core = lax.rem(gx, 2)
    z_low = lax.rem(lax.div(gx, 2), 2)
    y = lax.div(gx, 4)
    x = lax.div(gy, z_hi)
    z = lax.rem(gy, z_hi) * 2 + z_low

    def device(px, py, pz, pcore):
        return ((py * 2 + lax.rem(pz, 2)) * 2 + pcore, px * z_hi + lax.div(pz, 2))

    rank = y + core * (z - y)
    spot = x * ring + z + core * (y - z)
    group = lax.div(spot, part)
    slot = lax.rem(spot, part)
    partner = device(x, y, z, 1 - core)

    def on_ring(j):
        return device(x, y + (1 - core) * (j - y), z + core * (j - z), core)

    def on_plane(j):
        px, w = lax.div(j, ring), lax.rem(j, ring)
        return device(px, y + core * (w - y), z + (1 - core) * (w - z), core)

    def neighbour(dx, dy):
        return (lax.rem(gx + n_gx + dx, n_gx), lax.rem(gy + n_gy + dy, n_gy))

    def signal(where):
        pl.semaphore_signal(barrier, inc=1, device_id=where, device_id_type=MESH)

    barrier = pltpu.get_barrier_semaphore()
    sides = ((1, 0), (-1, 0), (0, 1), (0, -1), (1, 1), (1, -1), (-1, 1), (-1, -1))
    for side in sides:
        signal(neighbour(*side))
    signal(partner)

    @pl.loop(1, ring)
    def _(k):
        signal(on_ring(lax.rem(rank + k, ring)))

    @pl.loop(1, plane)
    def _(k):
        signal(on_plane(lax.rem(spot + k, plane)))

    def copy(source, target, send, recv, where):
        return pltpu.make_async_remote_copy(
            src_ref=source,
            dst_ref=target,
            send_sem=send,
            recv_sem=recv,
            device_id=where,
            device_id_type=MESH,
        )

    def halo(a, d):
        side = sides[d]
        if side[0] == 0:
            source = col.at[a, 1 if side[1] > 0 else 0]
        else:
            source = src.at[a, TX if side[0] > 0 else 1]
        landing = (0, TX + 1, TX + 2, TX + 3, TX + 4, TX + 5, TX + 6, TX + 7)[d]
        return copy(
            source, src.at[a, landing], halo_send.at[a, d], halo_recv.at[a, d], neighbour(*side)
        )

    edge_rows = iota((2 * TX, 1), 0)
    edges = onehot(jnp.where(edge_rows < TX, edge_rows * TY, (edge_rows - TX) * TY + TY - 1), (2 * TX, CELLS))

    def keep(a, value):
        src[a, 1 : TX + 1] = value.reshape(TX, TY, WIDE)
        col[a] = dot(edges, value).astype(BF16).reshape(2, TX, WIDE)

    rows256 = iota((256, 1), 0)
    to_columns = onehot(lax.rem(rows256, 64) * NZ + lax.div(rows256, 64), (256, 256))
    to_cells = onehot(lax.rem(rows256, NZ) * 64 + lax.div(rows256, NZ), (256, 256))

    def columns_of(ref):
        out = []
        for b in range(4):
            moved = dot(to_columns, ref[b * 256 : (b + 1) * 256, :])
            out.append(jnp.concatenate([moved[i * 64 : (i + 1) * 64] for i in range(NZ)], axis=1))
        return jnp.concatenate(out, axis=0).astype(BF16)

    keep(FIELD, columns_of(field_ref))
    keep(COT, columns_of(cot_ref))

    pl.semaphore_wait(barrier, len(sides) + 1 + (ring - 1) + (plane - 1))
    for a in (FIELD, COT):
        for d in range(8):
            halo(a, d).start()

    def build_band(layer, ref):
        nothing = jnp.zeros((64, 64), F32)
        for k in range(9):
            low, mid, high = (
                ref[:, (3 * k + i) * 64 : (3 * k + i + 1) * 64].astype(F32) for i in range(3)
            )
            lanes = slice((k % 3) * WIDE, (k % 3 + 1) * WIDE)
            for out_z, parts in enumerate(
                (
                    (mid, high, nothing, nothing),
                    (low, mid, high, nothing),
                    (nothing, low, mid, high),
                    (nothing, nothing, low, mid),
                )
            ):
                band[layer, k // 3, out_z * 64 : (out_z + 1) * 64, lanes] = jnp.concatenate(
                    parts, axis=1
                ).astype(BF16)

    build_band(0, first_ref)
    build_band(1, second_ref)

    framed_rows = (TX + 2) * TY
    source_rows = (TX + 8) * TY
    i = iota((framed_rows, 1), 0)
    r = lax.div(i, TY)
    c = lax.rem(i, TY)
    first_row, last_row = jnp.where(gx == 0, 0, -1), jnp.where(gx == n_gx - 1, TX + 1, -1)
    first_col, last_col = jnp.where(gy == 0, 0, -1), jnp.where(gy == n_gy - 1, TY - 1, -1)
    outside = (r == first_row) | (r == last_row)

    def shifted(step, at, column_slot, low_slot, high_slot, pick, outer):
        edge = jnp.where(
            r == 0,
            low_slot * TY + pick,
            jnp.where(r == TX + 1, high_slot * TY + pick, column_slot * TY + r - 1),
        )
        target = jnp.where(c == at, edge, i + step)
        return onehot(jnp.where(outside | (c == outer), -1, target), (framed_rows, source_rows))

    shift_low = shifted(-1, 0, TX + 2, TX + 4, TX + 6, TY - 1, first_col)
    shift_high = shifted(1, TY - 1, TX + 3, TX + 5, TX + 7, 0, last_col)
    above = jnp.where(gx == 0, 0.0, 1.0)
    below = jnp.where(gx == n_gx - 1, 0.0, 1.0)

    def frame(a):
        for d in range(8):
            halo(a, d).wait_recv()
        whole = src[a].reshape(source_rows, WIDE)
        cat[a, :, 0:WIDE] = dot(shift_low, whole).astype(BF16)
        cat[a, :, 2 * WIDE : 3 * WIDE] = dot(shift_high, whole).astype(BF16)
        cat[a, 0:TY, WIDE : 2 * WIDE] = (src[a, 0].astype(F32) * above).astype(BF16)
        cat[a, TY : TY + CELLS, WIDE : 2 * WIDE] = src[a, 1 : TX + 1].reshape(CELLS, WIDE)
        cat[a, TY + CELLS :, WIDE : 2 * WIDE] = (src[a, TX + 1].astype(F32) * below).astype(BF16)

    def rows_of(a, dx):
        return cat[a, dx * TY : dx * TY + CELLS, :]

    def convolve(a, layer):
        return sum(dot(rows_of(a, dx), band[layer, dx], NT) for dx in range(3))

    sample = samples_ref[...]
    sample_cell = jnp.broadcast_to(lax.div(sample, NZ).astype(F32), (256, 256)).T
    sample_level = jnp.broadcast_to(lax.rem(sample, NZ).astype(F32), (256, 256)).T
    lane = iota((256, 256), 1)
    gather = jnp.where(sample_cell == lane.astype(F32), 1.0, 0.0).astype(BF16)
    level = jnp.where(sample_level == lax.div(lane, C).astype(F32), 1.0, 0.0)
    low_lanes = iota((64, 128), 1) < 64

    frame(FIELD)
    hidden_pre = convolve(FIELD, 0)
    sigma = 1.0 / (1.0 + jnp.exp(-hidden_pre))
    keep(HIDDEN, (hidden_pre * sigma).astype(BF16))
    for d in range(8):
        halo(HIDDEN, d).start()

    frame(COT)
    back = jnp.zeros((CELLS, WIDE), F32)
    for dx in range(3):
        for dy in range(3):
            back += dot(
                cat[COT, dx * TY : dx * TY + CELLS, dy * WIDE : (dy + 1) * WIDE],
                band[1, 2 - dx, :, (2 - dy) * WIDE : (3 - dy) * WIDE],
            )
    delta = (back * sigma * (1.0 + hidden_pre * (1.0 - sigma))).astype(BF16)

    hidden = src[HIDDEN, 1 : TX + 1].reshape(CELLS, WIDE)
    delta_t = delta.astype(F32).T.astype(BF16)
    hidden_t = hidden.astype(F32).T.astype(BF16)
    for dx in range(3):
        grads[0, dx] = dot(delta_t, rows_of(FIELD, dx))
        grads[1, dx] = dot(hidden_t, rows_of(COT, dx))

    chunk = HALF // ring

    def place(k, value):
        half, rest = divmod(k * 64, HALF)
        at, row = divmod(rest, chunk)
        pay[half, at, row : row + 64, :] = value

    count = float(n_gx * n_gy * 256)
    scale = 1.0 / jnp.sqrt(jnp.float32(n_gx * n_gy * CELLS * NZ))

    def gram(values):
        picked = dot(gather, values) * level
        full_gram = dot(picked.T.astype(BF16), picked.astype(BF16))
        even = full_gram[0:64, 0:128] + full_gram[128:192, 128:256]
        odd = full_gram[64:128, 0:128] + full_gram[192:256, 128:256]
        return even, odd

    def two_grams(one, two):
        even, odd = gram(one)
        even2, odd2 = gram(two)
        return jnp.where(low_lanes, even + swap_halves(odd), swap_halves(even2) + odd2) / count

    field = src[FIELD, 1 : TX + 1].reshape(CELLS, WIDE)
    cot = src[COT, 1 : TX + 1].reshape(CELLS, WIDE)
    place(27, two_grams(field, cot))
    place(28, two_grams(hidden, delta))
    for k in range(29, BLOCKS):
        place(k, jnp.zeros((64, 128), F32))

    def pieces(layer, dx, dy):
        def piece(a, h):
            at = dy * WIDE + h * 128
            return grads[layer, dx, a * 64 : (a + 1) * 64, at : at + 128]

        return piece(0, 0) + piece(2, 1), piece(1, 0) + piece(3, 1), piece(2, 0), piece(1, 1)

    for dx in range(3):
        for dy in range(3):
            even, odd, before, after = pieces(0, dx, dy)
            even2, odd2, before2, after2 = pieces(1, 2 - dx, 2 - dy)
            swapped_even, swapped_odd = swap_halves(even), swap_halves(odd)
            swapped_even2, swapped_odd2 = swap_halves(even2), swap_halves(odd2)
            k = (dx * 3 + dy) * 3
            one = (odd + swap_halves(before), even + swapped_odd, after + swapped_even)
            two = (swap_halves(after2) + even2, swapped_even2 + odd2, swapped_odd2 + before2)
            for dz in range(3):
                place(k + dz, jnp.where(low_lanes, one[dz], two[dz]) * scale)

    def to_core(j):
        return copy(pay.at[1 - core, j], core_in.at[j], core_send.at[j], core_recv.at[j], partner)

    def to_ring(j):
        return copy(
            pay.at[core, j], axis_in.at[rank], axis_send.at[j], axis_recv.at[rank], on_ring(j)
        )

    def from_ring(j):
        return copy(pay.at[core, j], axis_in.at[j], axis_send.at[j], axis_recv.at[j], on_ring(j))

    def to_plane(j):
        return copy(
            plane_out.at[lax.rem(j, part)],
            plane_in.at[spot],
            plane_send.at[j],
            plane_recv.at[spot],
            on_plane(j),
        )

    def from_plane(j):
        return copy(
            plane_out.at[lax.rem(j, part)],
            plane_in.at[j],
            plane_send.at[j],
            plane_recv.at[j],
            on_plane(j),
        )

    def to_group(j):
        mine = full.at[core, rank, slot]
        return copy(
            mine, mine, gather_send.at[j], gather_recv.at[slot], on_plane(group * part + j)
        )

    def from_group(j):
        theirs = full.at[core, rank, j]
        return copy(
            theirs, theirs, gather_send.at[j], gather_recv.at[j], on_plane(group * part + j)
        )

    def spread(j):
        mine = full.at[core, rank]
        return copy(mine, mine, spread_send.at[j], spread_recv.at[rank], on_ring(j))

    def from_spread(j):
        theirs = full.at[core, j]
        return copy(theirs, theirs, spread_send.at[j], spread_recv.at[j], on_ring(j))

    def to_back(j):
        mine = full.at[core, j]
        return copy(mine, mine, back_send.at[j], back_recv.at[j], partner)

    def from_back(j):
        theirs = full.at[1 - core, j]
        return copy(theirs, theirs, back_send.at[j], back_recv.at[j], partner)

    partner_rank = z + core * (y - z)

    @pl.loop(1, ring + 1)
    def _(k):
        to_core(lax.rem(partner_rank + k, ring)).start()

    @pl.loop(1, ring)
    def _(k):
        j = lax.rem(rank + k, ring)
        to_core(j).wait_recv()
        pay[core, j] = pay[core, j] + core_in[j]
        to_ring(j).start()

    to_core(rank).wait_recv()
    axis_in[rank] = pay[core, rank] + core_in[rank]

    frame(HIDDEN)
    output = (field.astype(F32) + convolve(HIDDEN, 1)).astype(BF16).astype(F32)
    for b in range(4):
        block = output[b * 64 : (b + 1) * 64]
        stacked = jnp.concatenate([block[:, j * 64 : (j + 1) * 64] for j in range(NZ)], axis=0)
        out_ref[b * 256 : (b + 1) * 256, :] = dot(to_cells, stacked.astype(BF16)).astype(BF16)

    @pl.loop(1, ring)
    def _(k):
        from_ring(lax.rem(rank + ring - k, ring)).wait_recv()

    total = axis_in[0]
    for j in range(1, ring):
        total += axis_in[j]
    plane_out[...] = total.reshape(part, chunk // part, 128)

    @pl.loop(1, plane)
    def _(k):
        to_plane(lax.rem(spot + k, plane)).start()

    plane_in[spot] = plane_out[slot]

    @pl.loop(1, plane)
    def _(k):
        from_plane(lax.rem(spot + plane - k, plane)).wait_recv()

    full[core, rank, slot] = jnp.sum(plane_in[...], axis=0)

    @pl.loop(1, part)
    def _(k):
        to_group(lax.rem(slot + k, part)).start()

    @pl.loop(1, part)
    def _(k):
        from_group(lax.rem(slot + part - k, part)).wait_recv()

    @pl.loop(1, ring)
    def _(k):
        spread(lax.rem(rank + k, ring)).start()

    to_back(rank).start()

    @pl.loop(1, ring)
    def _(k):
        j = lax.rem(rank + ring - k, ring)
        from_spread(j).wait_recv()
        to_back(j).start()

    @pl.loop(0, ring)
    def _(j):
        from_back(j).wait_recv()

    def summed(k, n):
        half, rest = divmod(k * 64, HALF)
        at, row = divmod(rest, chunk)
        if n * 64 <= chunk - row:
            step = chunk // part
            if row % step == 0 and (n * 64) % step == 0:
                return full[half, at, row // step : (row + n * 64) // step].reshape(n * 64, 128)
        if n == 1:
            step = chunk // part
            return full[half, at, row // step, row % step : row % step + 64]
        return jnp.concatenate([summed(k + m, 1) for m in range(n)], axis=0)

    metric[...] = jnp.zeros((256, 256), F32)
    for m in range(4):
        lanes = slice((m // 2) * 128, (m // 2 + 1) * 128)
        block = summed(27 + m // 2, 1)
        mine = low_lanes if m % 2 == 0 else jnp.logical_not(low_lanes)
        metric[m * 64 : (m + 1) * 64, lanes] = jnp.where(mine, block, 0.0)
    eye = jnp.where(iota((256, 256), 0) == lane, 1.0, 0.0)
    matrix = metric[...] + 0.1 * eye
    norms = [
        jnp.sqrt(jnp.sum(matrix[m * 64 : (m + 1) * 64] * matrix[m * 64 : (m + 1) * 64]))
        for m in range(4)
    ]
    approx = jnp.concatenate([eye[m * 64 : (m + 1) * 64] / norms[m] for m in range(4)], axis=0)
    for _ in range(NS_ITERS):
        approx = dot32(approx, 2.0 * eye - dot32(matrix, approx))
    corner = approx[0:128, 0:128]
    right_second = jnp.where(low_lanes, 0.0, approx[64:128, 0:128])
    left_second = approx[128:192, 128:256]
    right_first = swap_halves(approx[192:256, 128:256])

    def four(block):
        low = jnp.where(low_lanes, block, 0.0)
        high = jnp.where(low_lanes, 0.0, swap_halves(block))
        none = jnp.zeros((64, 128), F32)
        return jnp.concatenate(
            [
                jnp.concatenate([low, none], axis=1),
                jnp.concatenate([high, none], axis=1),
                jnp.concatenate([none, low], axis=1),
                jnp.concatenate([none, high], axis=1),
            ],
            axis=0,
        )

    right_four = four(right_first)
    left_four = four(left_second)
    for q in range(7):
        block = summed(4 * q, 4)
        done = dot32(right_four, dot32(block, corner))
        lanes = jnp.concatenate([done[m * 64 : (m + 1) * 64, 0:64] for m in range(4)], axis=1)
        other = dot32(dot32(right_second, block, NT), left_four)
        width = 256 if q < 6 else 192
        first_out[:, q * 256 : q * 256 + width] = lanes[:, 0:width]
        second_out[:, q * 256 : q * 256 + width] = other[:, 0:width]

    for a in range(3):
        for d in range(8):
            halo(a, d).wait_send()

    @pl.loop(0, ring)
    def _(j):
        to_core(j).wait_send()
        to_back(j).wait_send()

    @pl.loop(1, ring)
    def _(k):
        j = lax.rem(rank + k, ring)
        to_ring(j).wait_send()
        spread(j).wait_send()

    @pl.loop(1, plane)
    def _(k):
        to_plane(lax.rem(spot + k, plane)).wait_send()

    @pl.loop(1, part)
    def _(k):
        to_group(lax.rem(slot + k, part)).wait_send()


def solution(mesh):
    n_gx, n_gy = mesh.shape["gx"], mesh.shape["gy"]
    ring = n_gx // 4
    z_hi = ring // 2
    plane = (n_gy // z_hi) * ring
    part = plane // 2
    chunk = HALF // ring
    vmem = pl.BlockSpec(memory_space=pltpu.VMEM)
    dma = pltpu.SemaphoreType.DMA

    def local(field, first_kernel, second_kernel, cotangent, samples):
        cells = field.shape[0] * field.shape[1] * field.shape[2]
        output, first, second = pl.pallas_call(
            functools.partial(kernel, (n_gx, n_gy, z_hi, ring, plane, part)),
            out_shape=(
                jax.ShapeDtypeStruct((cells, C), BF16),
                jax.ShapeDtypeStruct((C, 27 * C), F32),
                jax.ShapeDtypeStruct((C, 27 * C), F32),
            ),
            in_specs=[vmem] * 5,
            out_specs=(vmem,) * 3,
            scratch_shapes=[
                pltpu.VMEM((3, TX + 8, TY, WIDE), BF16),
                pltpu.VMEM((3, 2, TX, WIDE), BF16),
                pltpu.VMEM((3, (TX + 2) * TY, 3 * WIDE), BF16),
                pltpu.VMEM((2, 3, WIDE, 3 * WIDE), BF16),
                pltpu.VMEM((2, 3, WIDE, 3 * WIDE), F32),
                pltpu.VMEM((2, ring, chunk, 128), F32),
                pltpu.VMEM((ring, chunk, 128), F32),
                pltpu.VMEM((ring, chunk, 128), F32),
                pltpu.VMEM((part, chunk // part, 128), F32),
                pltpu.VMEM((plane, chunk // part, 128), F32),
                pltpu.VMEM((2, ring, part, chunk // part, 128), F32),
                pltpu.VMEM((256, 256), F32),
                dma((3, 8)),
                dma((3, 8)),
                dma((ring,)),
                dma((ring,)),
                dma((ring,)),
                dma((ring,)),
                dma((plane,)),
                dma((plane,)),
                dma((part,)),
                dma((part,)),
                dma((ring,)),
                dma((ring,)),
                dma((ring,)),
                dma((ring,)),
            ],
            compiler_params=pltpu.CompilerParams(
                collective_id=0, has_side_effects=True, vmem_limit_bytes=48 * 1024 * 1024
            ),
        )(
            field.reshape(cells, C),
            first_kernel.T,
            second_kernel.T,
            cotangent.reshape(cells, C),
            samples.reshape(1, -1),
        )
        return output.reshape(field.shape), first.T, second.T

    placed = (P("gx", "gy", None, None), P(), P(), P("gx", "gy", None, None), P("gx", "gy", None))
    return jax.shard_map(
        local,
        mesh=mesh,
        in_specs=placed,
        out_specs=(P("gx", "gy", None, None), P(), P()),
        check_vma=False,
    )
```

```python
import functools

import jax
import jax.numpy as jnp
from jax import lax
from jax.experimental import pallas as pl
from jax.experimental.pallas import tpu as pltpu
from jax.sharding import PartitionSpec as P

MESH = pl.DeviceIdType.MESH
F32 = jnp.float32
BF16 = jnp.bfloat16
NS_ITERS = 5
C = 64
TX = 16
TY = 16
NZ = 4
WIDE = NZ * C
CELLS = TX * TY
BLOCKS = 32
HALF = BLOCKS * 64 // 2
FIELD, COT, HIDDEN = 0, 1, 2
NN = (((1,), (0,)), ((), ()))
NT = (((1,), (1,)), ((), ()))


def dot(a, b, dims=NN):
    return lax.dot_general(a, b, dims, preferred_element_type=F32)


def split(value):
    high = value.astype(BF16)
    return high, (value - high.astype(F32)).astype(BF16)


def dot3(a, b):
    return dot(jnp.concatenate([a[0], a[0], a[1]], axis=1), jnp.concatenate([b[0], b[1], b[0]], axis=0))


def dot3_t(a, b):
    return dot(
        jnp.concatenate([a[0], a[0], a[1]], axis=1), jnp.concatenate([b[0], b[1], b[0]], axis=1), NT
    )


def iota(shape, dim):
    return lax.broadcasted_iota(jnp.int32, shape, dim)


def onehot(target, shape):
    return jnp.where(iota(shape, 1) == target, 1.0, 0.0).astype(BF16)


def swap_halves(value):
    return pltpu.roll(value, 64, 1)


def by_distance(count):
    return sorted(range(1, count), key=lambda k: -min(k, count - k))


def kernel(
    sizes,
    field_hbm,
    first_hbm,
    second_hbm,
    cot_hbm,
    samples_hbm,
    out_ref,
    first_out,
    second_out,
    field_ref,
    first_ref,
    second_ref,
    cot_ref,
    samples_ref,
    src,
    col,
    cat,
    band,
    grads,
    pay,
    core_in,
    one_in,
    two_out,
    two_in,
    x_in,
    whole,
    result,
    gram_pay,
    gram_core,
    gram_one,
    gram_two,
    gram_x,
    gram_all,
    metric,
    load_sem,
    halo_send,
    halo_recv,
    send_sems,
    recv_sems,
):
    n_gx, n_gy, z_hi, ring, n_x = sizes
    gx = lax.axis_index("gx")
    gy = lax.axis_index("gy")
    core = lax.rem(gx, 2)
    z_low = lax.rem(lax.div(gx, 2), 2)
    y = lax.div(gx, 4)
    x = lax.div(gy, z_hi)
    z = lax.rem(gy, z_hi) * 2 + z_low

    def load(k, source, target):
        return pltpu.make_async_copy(source, target, load_sem.at[k])

    loads = [
        load(k, *pair)
        for k, pair in enumerate(
            (
                (field_hbm, field_ref),
                (cot_hbm, cot_ref),
                (first_hbm, first_ref),
                (second_hbm, second_ref),
                (samples_hbm, samples_ref),
            )
        )
    ]
    for one in loads:
        one.start()

    rank = y + core * (z - y)
    rank_two = z + core * (y - z)
    partner = (gx + 1 - 2 * core, gy)

    def along_y(j):
        return gx + 4 * (j - y), gy

    def along_z(j):
        return gx + 2 * (lax.rem(j, 2) - z_low), x * z_hi + lax.div(j, 2)

    def on_ring(j):
        (ax, ay), (bx, by) = along_y(j), along_z(j)
        return (ax + core * (bx - ax), ay + core * (by - ay))

    def on_ring_two(j):
        (bx, by), (ax, ay) = along_y(j), along_z(j)
        return (ax + core * (bx - ax), ay + core * (by - ay))

    def along_x(j):
        return (gx, gy + z_hi * (j - x))

    def neighbour(dx, dy):
        return (lax.rem(gx + n_gx + dx, n_gx), lax.rem(gy + n_gy + dy, n_gy))

    barrier = pltpu.get_barrier_semaphore()

    def signal(where):
        pl.semaphore_signal(barrier, inc=1, device_id=where, device_id_type=MESH)

    sides = ((1, 0), (-1, 0), (0, 1), (0, -1), (1, 1), (1, -1), (-1, 1), (-1, -1))
    for side in sides:
        signal(neighbour(*side))
    signal(partner)
    for k in by_distance(ring):
        signal(on_ring(lax.rem(rank + k, ring)))
        signal(on_ring_two(lax.rem(rank_two + k, ring)))
    for k in range(1, n_x):
        signal(along_x(lax.rem(x + k, n_x)))

    def copy(source, target, send, recv, where):
        return pltpu.make_async_remote_copy(
            src_ref=source,
            dst_ref=target,
            send_sem=send,
            recv_sem=recv,
            device_id=where,
            device_id_type=MESH,
        )

    def halo(a, d):
        side = sides[d]
        if side[0] == 0:
            source = col.at[a, 1 if side[1] > 0 else 0]
        else:
            source = src.at[a, TX if side[0] > 0 else 1]
        landing = (0, TX + 1, TX + 2, TX + 3, TX + 4, TX + 5, TX + 6, TX + 7)[d]
        return copy(
            source, src.at[a, landing], halo_send.at[a, d], halo_recv.at[a, d], neighbour(*side)
        )

    class Exchange:
        def __init__(self, stage, count, me, where, source, target):
            self.stage, self.count, self.me, self.where = stage, count, me, where
            self.source, self.target = source, target
            self.order = by_distance(count)

        def outgoing(self, k):
            j = lax.rem(self.me + k, self.count)
            return copy(
                self.source(j),
                self.target(self.me),
                send_sems.at[self.stage, k],
                recv_sems.at[self.stage, k],
                self.where(j),
            )

        def sender(self, k):
            return lax.rem(self.me + self.count - k, self.count)

        def start(self):
            for k in self.order:
                self.outgoing(k).start()

        def arrived(self, k):
            there = self.target(self.sender(k))
            copy(
                there, there, send_sems.at[self.stage, k], recv_sems.at[self.stage, k], partner
            ).wait_recv()

        def wait(self):
            for k in reversed(self.order):
                self.arrived(k)

        def settle(self):
            for k in self.order:
                self.outgoing(k).wait_send()

    def to_core(layer, k):
        j = lax.rem(rank_two + k, ring)
        return copy(
            pay.at[layer, 1 - core, j],
            core_in.at[layer, j],
            send_sems.at[12 * layer, k],
            recv_sems.at[12 * layer, k],
            partner,
        )

    def from_core(layer, k):
        j = lax.rem(rank + k, ring)
        return copy(
            pay.at[layer, core, j],
            core_in.at[layer, j],
            send_sems.at[12 * layer, k],
            recv_sems.at[12 * layer, k],
            partner,
        )

    def to_back(k):
        there = result.at[core, lax.rem(rank + ring - k, ring)]
        return copy(there, there, send_sems.at[1, k], recv_sems.at[1, k], partner)

    def from_back(k):
        there = result.at[1 - core, lax.rem(rank_two + ring - k, ring)]
        return copy(there, there, send_sems.at[1, k], recv_sems.at[1, k], partner)

    ones = [
        Exchange(
            stage,
            ring,
            rank,
            on_ring,
            functools.partial(lambda layer, j: pay.at[layer, core, j], layer),
            functools.partial(lambda layer, j: one_in.at[layer, j], layer),
        )
        for layer, stage in enumerate((2, 13))
    ]
    two = Exchange(3, ring, rank_two, on_ring_two, lambda j: two_out.at[j], lambda j: two_in.at[j])
    third = Exchange(4, n_x, x, along_x, lambda j: x_in.at[x], lambda j: x_in.at[j])
    gather_two = Exchange(
        5, ring, rank_two, on_ring_two, lambda j: whole.at[rank_two], lambda j: whole.at[j]
    )
    spread = Exchange(
        6, ring, rank, on_ring, lambda j: result.at[core, rank], lambda j: result.at[core, j]
    )
    gram_to_core = copy(
        gram_pay.at[1 - core], gram_core, send_sems.at[7, 0], recv_sems.at[7, 0], partner
    )
    gram_first = Exchange(
        8, ring, rank, on_ring, lambda j: gram_pay.at[core, j], lambda j: gram_one.at[j]
    )
    gram_second = Exchange(
        9, ring, rank_two, on_ring_two, lambda j: gram_two.at[rank_two], lambda j: gram_two.at[j]
    )
    gram_third = Exchange(10, n_x, x, along_x, lambda j: gram_x.at[x], lambda j: gram_x.at[j])
    gram_gather = Exchange(
        11, ring, rank, on_ring, lambda j: gram_all.at[core, rank], lambda j: gram_all.at[core, j]
    )
    gram_back = copy(
        gram_all.at[core], gram_all.at[core], send_sems.at[7, 1], recv_sems.at[7, 1], partner
    )
    gram_from_back = copy(
        gram_all.at[1 - core], gram_all.at[1 - core], send_sems.at[7, 1], recv_sems.at[7, 1], partner
    )

    edge_rows = iota((2 * TX, 1), 0)
    edges = onehot(jnp.where(edge_rows < TX, edge_rows * TY, (edge_rows - TX) * TY + TY - 1), (2 * TX, CELLS))

    def keep(a, value):
        src[a, 1 : TX + 1] = value.reshape(TX, TY, WIDE)
        col[a] = dot(edges, value).astype(BF16).reshape(2, TX, WIDE)

    rows256 = iota((256, 1), 0)
    to_columns = onehot(lax.rem(rows256, 64) * NZ + lax.div(rows256, 64), (256, 256))
    to_cells = onehot(lax.rem(rows256, NZ) * 64 + lax.div(rows256, NZ), (256, 256))

    def columns_of(ref):
        out = []
        for b in range(4):
            moved = dot(to_columns, ref[b * 256 : (b + 1) * 256, :])
            out.append(jnp.concatenate([moved[i * 64 : (i + 1) * 64] for i in range(NZ)], axis=1))
        return jnp.concatenate(out, axis=0).astype(BF16)

    loads[0].wait()
    keep(FIELD, columns_of(field_ref))
    loads[1].wait()
    keep(COT, columns_of(cot_ref))
    pl.semaphore_wait(barrier, len(sides) + 1 + 2 * (ring - 1) + n_x - 1)
    for d in range(8):
        halo(FIELD, d).start()
    for d in range(8):
        halo(COT, d).start()

    def build_band(layer, ref):
        nothing = jnp.zeros((64, 64), F32)
        for k in range(9):
            low, mid, high = (
                ref[:, (3 * k + i) * 64 : (3 * k + i + 1) * 64].astype(F32) for i in range(3)
            )
            lanes = slice((k % 3) * WIDE, (k % 3 + 1) * WIDE)
            for out_z, parts in enumerate(
                (
                    (mid, high, nothing, nothing),
                    (low, mid, high, nothing),
                    (nothing, low, mid, high),
                    (nothing, nothing, low, mid),
                )
            ):
                band[layer, k // 3, out_z * 64 : (out_z + 1) * 64, lanes] = jnp.concatenate(
                    parts, axis=1
                ).astype(BF16)

    loads[2].wait()
    build_band(0, first_ref)
    loads[3].wait()
    build_band(1, second_ref)
    loads[4].wait()
    framed_rows = (TX + 2) * TY
    source_rows = (TX + 8) * TY
    i = iota((framed_rows, 1), 0)
    r = lax.div(i, TY)
    c = lax.rem(i, TY)
    first_row, last_row = jnp.where(gx == 0, 0, -1), jnp.where(gx == n_gx - 1, TX + 1, -1)
    first_col, last_col = jnp.where(gy == 0, 0, -1), jnp.where(gy == n_gy - 1, TY - 1, -1)
    outside = (r == first_row) | (r == last_row)

    def shifted(step, at, column_slot, low_slot, high_slot, pick, outer):
        edge = jnp.where(
            r == 0,
            low_slot * TY + pick,
            jnp.where(r == TX + 1, high_slot * TY + pick, column_slot * TY + r - 1),
        )
        target = jnp.where(c == at, edge, i + step)
        return onehot(jnp.where(outside | (c == outer), -1, target), (framed_rows, source_rows))

    shift_low = shifted(-1, 0, TX + 2, TX + 4, TX + 6, TY - 1, first_col)
    shift_high = shifted(1, TY - 1, TX + 3, TX + 5, TX + 7, 0, last_col)
    above = jnp.where(gx == 0, 0.0, 1.0)
    below = jnp.where(gx == n_gx - 1, 0.0, 1.0)

    def frame(a):
        for d in range(8):
            halo(a, d).wait_recv()
        whole = src[a].reshape(source_rows, WIDE)
        cat[a, :, 0:WIDE] = dot(shift_low, whole).astype(BF16)
        cat[a, :, 2 * WIDE : 3 * WIDE] = dot(shift_high, whole).astype(BF16)
        cat[a, 0:TY, WIDE : 2 * WIDE] = (src[a, 0].astype(F32) * above).astype(BF16)
        cat[a, TY : TY + CELLS, WIDE : 2 * WIDE] = src[a, 1 : TX + 1].reshape(CELLS, WIDE)
        cat[a, TY + CELLS :, WIDE : 2 * WIDE] = (src[a, TX + 1].astype(F32) * below).astype(BF16)

    def rows_of(a, dx):
        return cat[a, dx * TY : dx * TY + CELLS, :]

    def convolve(a, layer):
        return sum(dot(rows_of(a, dx), band[layer, dx], NT) for dx in range(3))

    sample = samples_ref[...]
    sample_cell = jnp.broadcast_to(lax.div(sample, NZ).astype(F32), (256, 256)).T
    sample_level = jnp.broadcast_to(lax.rem(sample, NZ).astype(F32), (256, 256)).T
    lane = iota((256, 256), 1)
    gather = jnp.where(sample_cell == lane.astype(F32), 1.0, 0.0).astype(BF16)
    level = jnp.where(sample_level == lax.div(lane, C).astype(F32), 1.0, 0.0)
    low_lanes = iota((64, 128), 1) < 64

    def gram(values):
        picked = dot(gather, values) * level
        full_gram = dot(picked.T.astype(BF16), picked.astype(BF16))
        even = full_gram[0:64, 0:128] + full_gram[128:192, 128:256]
        odd = full_gram[64:128, 0:128] + full_gram[192:256, 128:256]
        return even, odd

    count = float(n_gx * n_gy * 256)
    scale = 1.0 / jnp.sqrt(jnp.float32(n_gx * n_gy * CELLS * NZ))
    gram_rows = 64 // ring

    def two_grams(one, two):
        even, odd = gram(one)
        even2, odd2 = gram(two)
        both = jnp.where(low_lanes, even + swap_halves(odd), swap_halves(even2) + odd2)
        return (both / count).reshape(ring, gram_rows, 128)

    field = src[FIELD, 1 : TX + 1].reshape(CELLS, WIDE)
    cot = src[COT, 1 : TX + 1].reshape(CELLS, WIDE)
    gram_pay[0] = two_grams(field, cot)

    chunk = HALF // ring

    def assemble(layer, flip):
        taps = [None] * 27
        for dx in range(3):
            for dy in range(3):

                def piece(a, h):
                    at = dy * WIDE + h * 128
                    return grads[layer, dx, a * 64 : (a + 1) * 64, at : at + 128]

                even, odd = piece(0, 0) + piece(2, 1), piece(1, 0) + piece(3, 1)
                pairs = ((odd, piece(2, 0)), (even, odd), (piece(1, 1), even))
                for e in range(3):
                    tap = (dx * 3 + dy) * 3 + e
                    taps[26 - tap if flip else tap] = pairs[e]
        for k in range(BLOCKS // 2):
            low, high = 2 * k, 2 * k + 1
            value = jnp.zeros((64, 128), F32)
            if low < 27:
                value = jnp.where(low_lanes, taps[low][0] + swap_halves(taps[low][1]), 0.0) * scale
            if high < 27:
                other = (swap_halves(taps[high][0]) + taps[high][1]) * scale
                value = jnp.where(low_lanes, value, other)
            per = chunk // 128
            half, rest = divmod(k, ring * per)
            at, p = divmod(rest, per)
            pay[layer, half, at, p * 64 : (p + 1) * 64, :] = value

    def send_on(layer):
        for k in ones[layer].order:
            from_core(layer, k).wait_recv()
            j = lax.rem(rank + k, ring)
            pay[layer, core, j] = pay[layer, core, j] + core_in[layer, j]
            ones[layer].outgoing(k).start()
        from_core(layer, 0).wait_recv()
        one_in[layer, rank] = pay[layer, core, rank] + core_in[layer, rank]

    frame(FIELD)
    hidden_pre = convolve(FIELD, 0)
    sigma = 1.0 / (1.0 + jnp.exp(-hidden_pre))
    hidden = (hidden_pre * sigma).astype(BF16)
    keep(HIDDEN, hidden)
    for d in range(8):
        halo(HIDDEN, d).start()

    frame(COT)
    hidden_t = hidden.astype(F32).T.astype(BF16)
    for dx in range(3):
        grads[1, dx] = dot(hidden_t, rows_of(COT, dx))
    assemble(1, True)
    for k in ones[1].order + [0]:
        to_core(1, k).start()

    back = jnp.zeros((CELLS, WIDE), F32)
    for dx in range(3):
        for dy in range(3):
            back += dot(
                cat[COT, dx * TY : dx * TY + CELLS, dy * WIDE : (dy + 1) * WIDE],
                band[1, 2 - dx, :, (2 - dy) * WIDE : (3 - dy) * WIDE],
            )
    delta = (back * sigma * (1.0 + hidden_pre * (1.0 - sigma))).astype(BF16)
    gram_pay[1] = two_grams(hidden, delta)
    gram_to_core.start()
    send_on(1)

    delta_t = delta.astype(F32).T.astype(BF16)
    for dx in range(3):
        grads[0, dx] = dot(delta_t, rows_of(FIELD, dx))
    gram_to_core.wait_recv()
    gram_pay[core] = gram_pay[core] + gram_core[...]
    gram_one[rank] = gram_pay[core, rank]
    gram_first.start()
    assemble(0, False)
    for k in ones[0].order + [0]:
        to_core(0, k).start()
    send_on(0)

    gram_first.wait()
    gram_two[rank_two] = jnp.sum(gram_one[...], axis=0)
    gram_second.start()

    frame(HIDDEN)
    output = (field.astype(F32) + convolve(HIDDEN, 1)).astype(BF16).astype(F32)
    for b in range(4):
        block = output[b * 64 : (b + 1) * 64]
        stacked = jnp.concatenate([block[:, j * 64 : (j + 1) * 64] for j in range(NZ)], axis=0)
        out_ref[b * 256 : (b + 1) * 256, :] = dot(to_cells, stacked.astype(BF16)).astype(BF16)

    gram_second.wait()
    gram_x[x] = jnp.sum(gram_two[...], axis=0)
    gram_third.start()

    part = chunk // 2 // ring
    for layer in range(2):
        ones[layer].wait()
        total = one_in[layer, 0]
        for j in range(1, ring):
            total += one_in[layer, j]
        two_out[:, layer * part : (layer + 1) * part] = total.reshape(ring, part, 128)
    two_in[rank_two] = two_out[rank_two]
    two.start()
    for a in range(3):
        for d in range(8):
            halo(a, d).wait_send()

    gram_third.wait()
    gram_all[core, rank] = jnp.sum(gram_x[...], axis=0)
    gram_gather.start()
    gram_to_core.wait_send()
    for k in range(ring):
        to_core(1, k).wait_send()
        to_core(0, k).wait_send()

    two.wait()
    x_in[x] = jnp.sum(two_in[...], axis=0)
    third.start()
    for stage in (ones[1], ones[0], gram_first):
        stage.settle()
    gram_gather.wait()
    gram_back.start()

    third.wait()
    whole[rank_two] = jnp.sum(x_in[...], axis=0)
    gather_two.start()

    gram_from_back.wait_recv()
    metric[...] = jnp.zeros((256, 256), F32)
    for m in range(4):
        lanes = slice((m // 2) * 128, (m // 2 + 1) * 128)
        mine = low_lanes if m % 2 == 0 else jnp.logical_not(low_lanes)
        block = gram_all[m // 2].reshape(64, 128)
        metric[m * 64 : (m + 1) * 64, lanes] = jnp.where(mine, block, 0.0)
    eye = jnp.where(iota((256, 256), 0) == lane, 1.0, 0.0)
    matrix = metric[...] + 0.1 * eye
    norms = [
        jnp.sqrt(jnp.sum(matrix[m * 64 : (m + 1) * 64] * matrix[m * 64 : (m + 1) * 64]))
        for m in range(4)
    ]
    approx = jnp.concatenate([eye[m * 64 : (m + 1) * 64] / norms[m] for m in range(4)], axis=0)
    matrix = split(matrix)

    def refine(value):
        parts = split(value)
        return dot3(parts, split(2.0 * eye - dot3(matrix, parts)))

    for _ in range(NS_ITERS):
        approx = refine(approx)

    def twice(block, low):
        other = swap_halves(block)
        first, second = (block, other) if low else (other, block)
        return split(
            jnp.concatenate(
                [jnp.where(low_lanes, first, 0.0), jnp.where(low_lanes, 0.0, second)], axis=0
            )
        )

    left_first = twice(approx[0:64, 0:128], True)
    right_second = twice(approx[64:128, 0:128], False)
    none = jnp.zeros((64, 128), F32)
    left_second = split(
        jnp.concatenate([jnp.where(low_lanes, approx[128:192, 128:256], 0.0), none], axis=0)
    )
    right_first = split(
        jnp.where(low_lanes, swap_halves(approx[192:256, 128:256]), 0.0)
    )

    for stage in (two, third, gram_second, gram_third, gram_gather):
        stage.settle()
    gram_back.wait_send()
    gather_two.wait()
    pairs = chunk // 128
    both = [
        whole[:, layer * part : (layer + 1) * part].reshape(pairs, 64, 128) for layer in range(2)
    ]
    for p in range(pairs):
        block = split(jnp.concatenate([both[0][p], none], axis=0))
        result[core, rank, p, 0:64, :] = dot3(
            right_first, split(dot3(block, left_first))
        ).astype(BF16)
        block = split(jnp.concatenate([both[1][p], none], axis=0))
        done = dot3(split(dot3_t(right_second, block)), left_second)
        result[core, rank, p, 64:128, :] = jnp.where(
            low_lanes, done[0:64], swap_halves(done[64:128])
        ).astype(BF16)
    spread.start()
    to_back(0).start()
    for k in reversed(spread.order):
        spread.arrived(k)
        to_back(k).start()
    for k in [0] + spread.order[::-1]:
        from_back(k).wait_recv()

    for k in range(14):
        half, rest = divmod(k, HALF // 128)
        at, p = divmod(rest, pairs)
        lanes = 128 if k < 13 else 64
        first_out[:, k * 128 : k * 128 + lanes] = result[half, at, p, 0:64, 0:lanes]
        second_out[:, k * 128 : k * 128 + lanes] = result[half, at, p, 64:128, 0:lanes]

    for k in range(ring):
        to_back(k).wait_send()
    gather_two.settle()
    spread.settle()


def solution(mesh):
    n_gx, n_gy = mesh.shape["gx"], mesh.shape["gy"]
    ring = n_gx // 4
    z_hi = ring // 2
    n_x = n_gy // z_hi
    chunk = HALF // ring
    most = max(ring, n_x)
    vmem = pl.BlockSpec(memory_space=pltpu.VMEM)
    anywhere = pl.BlockSpec(memory_space=pl.ANY)
    dma = pltpu.SemaphoreType.DMA

    def local(field, first_kernel, second_kernel, cotangent, samples):
        cells = field.shape[0] * field.shape[1] * field.shape[2]
        output, first, second = pl.pallas_call(
            functools.partial(kernel, (n_gx, n_gy, z_hi, ring, n_x)),
            out_shape=(
                jax.ShapeDtypeStruct((cells, C), BF16),
                jax.ShapeDtypeStruct((C, 27 * C), BF16),
                jax.ShapeDtypeStruct((C, 27 * C), BF16),
            ),
            in_specs=[anywhere] * 5,
            out_specs=(vmem,) * 3,
            scratch_shapes=[
                pltpu.VMEM((cells, C), BF16),
                pltpu.VMEM((C, 27 * C), BF16),
                pltpu.VMEM((C, 27 * C), BF16),
                pltpu.VMEM((cells, C), BF16),
                pltpu.VMEM((1, 256), jnp.int32),
                pltpu.VMEM((3, TX + 8, TY, WIDE), BF16),
                pltpu.VMEM((3, 2, TX, WIDE), BF16),
                pltpu.VMEM((3, (TX + 2) * TY, 3 * WIDE), BF16),
                pltpu.VMEM((2, 3, WIDE, 3 * WIDE), BF16),
                pltpu.VMEM((2, 3, WIDE, 3 * WIDE), F32),
                pltpu.VMEM((2, 2, ring, chunk // 2, 128), F32),
                pltpu.VMEM((2, ring, chunk // 2, 128), F32),
                pltpu.VMEM((2, ring, chunk // 2, 128), F32),
                pltpu.VMEM((ring, chunk // ring, 128), F32),
                pltpu.VMEM((ring, chunk // ring, 128), F32),
                pltpu.VMEM((n_x, chunk // ring, 128), F32),
                pltpu.VMEM((ring, chunk // ring, 128), F32),
                pltpu.VMEM((2, ring, chunk // 128, 128, 128), BF16),
                pltpu.VMEM((2, ring, 64 // ring, 128), F32),
                pltpu.VMEM((ring, 64 // ring, 128), F32),
                pltpu.VMEM((ring, 64 // ring, 128), F32),
                pltpu.VMEM((ring, 64 // ring, 128), F32),
                pltpu.VMEM((n_x, 64 // ring, 128), F32),
                pltpu.VMEM((2, ring, 64 // ring, 128), F32),
                pltpu.VMEM((256, 256), F32),
                dma((5,)),
                dma((3, 8)),
                dma((3, 8)),
                dma((14, most)),
                dma((14, most)),
            ],
            compiler_params=pltpu.CompilerParams(
                collective_id=0, has_side_effects=True, vmem_limit_bytes=54 * 1024 * 1024
            ),
        )(
            field.reshape(cells, C),
            first_kernel.T,
            second_kernel.T,
            cotangent.reshape(cells, C),
            samples.reshape(1, -1),
        )
        return output.reshape(field.shape), first.astype(F32).T, second.astype(F32).T

    placed = (P("gx", "gy", None, None), P(), P(), P("gx", "gy", None, None), P("gx", "gy", None))
    return jax.shard_map(
        local,
        mesh=mesh,
        in_specs=placed,
        out_specs=(P("gx", "gy", None, None), P(), P()),
        check_vma=False,
    )
```

```python
import functools

import jax
import jax.numpy as jnp
from jax import lax
from jax.experimental import pallas as pl
from jax.experimental.pallas import tpu as pltpu
from jax.sharding import PartitionSpec as P

MESH = pl.DeviceIdType.MESH
F32 = jnp.float32
BF16 = jnp.bfloat16
NS_ITERS = 5
C = 64
TX = 16
TY = 16
NZ = 4
WIDE = NZ * C
CELLS = TX * TY
BLOCKS = 32
HALF = BLOCKS * 64 // 2
FIELD, COT, HIDDEN = 0, 1, 2
NN = (((1,), (0,)), ((), ()))
NT = (((1,), (1,)), ((), ()))


def dot(a, b, dims=NN):
    return lax.dot_general(a, b, dims, preferred_element_type=F32)


def split(value):
    high = value.astype(BF16)
    return high, (value - high.astype(F32)).astype(BF16)


def dot3(a, b):
    return dot(jnp.concatenate([a[0], a[0], a[1]], axis=1), jnp.concatenate([b[0], b[1], b[0]], axis=0))


def dot3_t(a, b):
    return dot(
        jnp.concatenate([a[0], a[0], a[1]], axis=1), jnp.concatenate([b[0], b[1], b[0]], axis=1), NT
    )


def iota(shape, dim):
    return lax.broadcasted_iota(jnp.int32, shape, dim)


def onehot(target, shape):
    return jnp.where(iota(shape, 1) == target, 1.0, 0.0).astype(BF16)


def swap_halves(value):
    return pltpu.roll(value, 64, 1)


def by_distance(count):
    return sorted(range(1, count), key=lambda k: -min(k, count - k))


def kernel(
    sizes,
    field_hbm,
    first_hbm,
    second_hbm,
    cot_hbm,
    samples_hbm,
    out_hbm,
    first_out,
    second_out,
    field_ref,
    first_ref,
    second_ref,
    cot_ref,
    samples_ref,
    out_ref,
    src,
    col,
    cat,
    band,
    grads,
    pay,
    core_in,
    one_in,
    two_out,
    two_in,
    x_in,
    whole,
    result,
    gram_pay,
    gram_one,
    gram_two,
    gram_x,
    gram_all,
    metric,
    load_sem,
    store_sem,
    halo_send,
    halo_recv,
    send_sems,
    recv_sems,
):
    n_gx, n_gy, z_hi, ring, n_x = sizes
    gx = lax.axis_index("gx")
    gy = lax.axis_index("gy")
    core = lax.rem(gx, 2)
    z_low = lax.rem(lax.div(gx, 2), 2)
    y = lax.div(gx, 4)
    x = lax.div(gy, z_hi)
    z = lax.rem(gy, z_hi) * 2 + z_low

    def load(k, source, target):
        return pltpu.make_async_copy(source, target, load_sem.at[k])

    loads = [
        load(k, *pair)
        for k, pair in enumerate(
            (
                (field_hbm, field_ref),
                (cot_hbm, cot_ref),
                (first_hbm, first_ref),
                (second_hbm, second_ref),
                (samples_hbm, samples_ref),
            )
        )
    ]
    for one in loads:
        one.start()

    rank = y + core * (z - y)
    rank_two = z + core * (y - z)
    partner = (gx + 1 - 2 * core, gy)

    def along_y(j):
        return gx + 4 * (j - y), gy

    def along_z(j):
        return gx + 2 * (lax.rem(j, 2) - z_low), x * z_hi + lax.div(j, 2)

    def on_ring(j):
        (ax, ay), (bx, by) = along_y(j), along_z(j)
        return (ax + core * (bx - ax), ay + core * (by - ay))

    def on_ring_two(j):
        (bx, by), (ax, ay) = along_y(j), along_z(j)
        return (ax + core * (bx - ax), ay + core * (by - ay))

    def along_x(j):
        return (gx, gy + z_hi * (j - x))

    seat = x * 2 + core

    def along_seats(j):
        return (gx + lax.rem(j, 2) - core, gy + z_hi * (lax.div(j, 2) - x))

    def neighbour(dx, dy):
        return (lax.rem(gx + n_gx + dx, n_gx), lax.rem(gy + n_gy + dy, n_gy))

    barrier = pltpu.get_barrier_semaphore()

    def signal(where):
        pl.semaphore_signal(barrier, inc=1, device_id=where, device_id_type=MESH)

    sides = ((1, 0), (-1, 0), (0, 1), (0, -1), (1, 1), (1, -1), (-1, 1), (-1, -1))
    for side in sides:
        signal(neighbour(*side))
    for k in by_distance(ring):
        signal(on_ring(lax.rem(rank + k, ring)))
        signal(on_ring_two(lax.rem(rank_two + k, ring)))
    for k in range(1, 2 * n_x):
        signal(along_seats(lax.rem(seat + k, 2 * n_x)))

    def copy(source, target, send, recv, where):
        return pltpu.make_async_remote_copy(
            src_ref=source,
            dst_ref=target,
            send_sem=send,
            recv_sem=recv,
            device_id=where,
            device_id_type=MESH,
        )

    def halo(a, d):
        side = sides[d]
        if side[0] == 0:
            source = col.at[a, 1 if side[1] > 0 else 0]
        else:
            source = src.at[a, TX if side[0] > 0 else 1]
        landing = (0, TX + 1, TX + 2, TX + 3, TX + 4, TX + 5, TX + 6, TX + 7)[d]
        return copy(
            source, src.at[a, landing], halo_send.at[a, d], halo_recv.at[a, d], neighbour(*side)
        )

    class Exchange:
        def __init__(self, stage, count, me, where, source, target):
            self.stage, self.count, self.me, self.where = stage, count, me, where
            self.source, self.target = source, target
            self.order = by_distance(count)

        def outgoing(self, k):
            j = lax.rem(self.me + k, self.count)
            return copy(
                self.source(j),
                self.target(self.me),
                send_sems.at[self.stage, k],
                recv_sems.at[self.stage, k],
                self.where(j),
            )

        def sender(self, k):
            return lax.rem(self.me + self.count - k, self.count)

        def start(self):
            for k in self.order:
                self.outgoing(k).start()

        def arrived(self, k):
            there = self.target(self.sender(k))
            copy(
                there, there, send_sems.at[self.stage, k], recv_sems.at[self.stage, k], partner
            ).wait_recv()

        def wait(self):
            for k in reversed(self.order):
                self.arrived(k)

        def settle(self):
            for k in self.order:
                self.outgoing(k).wait_send()

    def to_core(layer, k):
        j = lax.rem(rank_two + k, ring)
        return copy(
            pay.at[layer, 1 - core, j],
            core_in.at[layer, j],
            send_sems.at[12 * layer, k],
            recv_sems.at[12 * layer, k],
            partner,
        )

    def from_core(layer, k):
        j = lax.rem(rank + k, ring)
        return copy(
            pay.at[layer, core, j],
            core_in.at[layer, j],
            send_sems.at[12 * layer, k],
            recv_sems.at[12 * layer, k],
            partner,
        )

    def to_back(k):
        there = result.at[core, lax.rem(rank + ring - k, ring)]
        return copy(there, there, send_sems.at[1, k], recv_sems.at[1, k], partner)

    def from_back(k):
        there = result.at[1 - core, lax.rem(rank_two + ring - k, ring)]
        return copy(there, there, send_sems.at[1, k], recv_sems.at[1, k], partner)

    ones = [
        Exchange(
            stage,
            ring,
            rank,
            on_ring,
            functools.partial(lambda layer, j: pay.at[layer, core, j], layer),
            functools.partial(lambda layer, j: one_in.at[layer, j], layer),
        )
        for layer, stage in enumerate((2, 13))
    ]
    two = Exchange(3, ring, rank_two, on_ring_two, lambda j: two_out.at[j], lambda j: two_in.at[j])
    third = Exchange(4, n_x, x, along_x, lambda j: x_in.at[x], lambda j: x_in.at[j])
    gather_two = Exchange(
        5, ring, rank_two, on_ring_two, lambda j: whole.at[rank_two], lambda j: whole.at[j]
    )
    spread = Exchange(
        6, ring, rank, on_ring, lambda j: result.at[core, rank], lambda j: result.at[core, j]
    )
    gram_first = Exchange(
        8, ring, y, along_y, lambda j: gram_pay.at[j], lambda j: gram_one.at[j]
    )
    gram_second = Exchange(
        9, ring, z, along_z, lambda j: gram_two.at[z], lambda j: gram_two.at[j]
    )
    gram_third = Exchange(
        10, 2 * n_x, seat, along_seats, lambda j: gram_x.at[seat], lambda j: gram_x.at[j]
    )
    gram_gather = Exchange(
        11, ring, y, along_y, lambda j: gram_all.at[y], lambda j: gram_all.at[j]
    )

    edge_rows = iota((2 * TX, 1), 0)
    edges = onehot(jnp.where(edge_rows < TX, edge_rows * TY, (edge_rows - TX) * TY + TY - 1), (2 * TX, CELLS))

    def keep(a, value):
        src[a, 1 : TX + 1] = value.reshape(TX, TY, WIDE)
        col[a] = dot(edges, value).astype(BF16).reshape(2, TX, WIDE)

    rows256 = iota((256, 1), 0)
    to_columns = onehot(lax.rem(rows256, 64) * NZ + lax.div(rows256, 64), (256, 256))
    to_cells = onehot(lax.rem(rows256, NZ) * 64 + lax.div(rows256, NZ), (256, 256))

    def columns_of(ref):
        out = []
        for b in range(4):
            moved = dot(to_columns, ref[b * 256 : (b + 1) * 256, :])
            out.append(jnp.concatenate([moved[i * 64 : (i + 1) * 64] for i in range(NZ)], axis=1))
        return jnp.concatenate(out, axis=0).astype(BF16)

    loads[0].wait()
    keep(FIELD, columns_of(field_ref))
    loads[1].wait()
    keep(COT, columns_of(cot_ref))
    pl.semaphore_wait(barrier, len(sides) + 2 * (ring - 1) + 2 * n_x - 1)
    for d in range(8):
        halo(FIELD, d).start()
    for d in range(8):
        halo(COT, d).start()

    def build_band(layer, ref):
        nothing = jnp.zeros((64, 64), F32)
        for k in range(9):
            low, mid, high = (
                ref[:, (3 * k + i) * 64 : (3 * k + i + 1) * 64].astype(F32) for i in range(3)
            )
            lanes = slice((k % 3) * WIDE, (k % 3 + 1) * WIDE)
            for out_z, parts in enumerate(
                (
                    (mid, high, nothing, nothing),
                    (low, mid, high, nothing),
                    (nothing, low, mid, high),
                    (nothing, nothing, low, mid),
                )
            ):
                band[layer, k // 3, out_z * 64 : (out_z + 1) * 64, lanes] = jnp.concatenate(
                    parts, axis=1
                ).astype(BF16)

    loads[2].wait()
    build_band(0, first_ref)
    loads[3].wait()
    build_band(1, second_ref)
    loads[4].wait()
    framed_rows = (TX + 2) * TY
    source_rows = (TX + 8) * TY
    i = iota((framed_rows, 1), 0)
    r = lax.div(i, TY)
    c = lax.rem(i, TY)
    first_row, last_row = jnp.where(gx == 0, 0, -1), jnp.where(gx == n_gx - 1, TX + 1, -1)
    first_col, last_col = jnp.where(gy == 0, 0, -1), jnp.where(gy == n_gy - 1, TY - 1, -1)
    outside = (r == first_row) | (r == last_row)

    def shifted(step, at, column_slot, low_slot, high_slot, pick, outer):
        edge = jnp.where(
            r == 0,
            low_slot * TY + pick,
            jnp.where(r == TX + 1, high_slot * TY + pick, column_slot * TY + r - 1),
        )
        target = jnp.where(c == at, edge, i + step)
        return onehot(jnp.where(outside | (c == outer), -1, target), (framed_rows, source_rows))

    shift_low = shifted(-1, 0, TX + 2, TX + 4, TX + 6, TY - 1, first_col)
    shift_high = shifted(1, TY - 1, TX + 3, TX + 5, TX + 7, 0, last_col)
    above = jnp.where(gx == 0, 0.0, 1.0)
    below = jnp.where(gx == n_gx - 1, 0.0, 1.0)

    def frame(a):
        for d in range(8):
            halo(a, d).wait_recv()
        whole = src[a].reshape(source_rows, WIDE)
        cat[a, :, 0:WIDE] = dot(shift_low, whole).astype(BF16)
        cat[a, :, 2 * WIDE : 3 * WIDE] = dot(shift_high, whole).astype(BF16)
        cat[a, 0:TY, WIDE : 2 * WIDE] = (src[a, 0].astype(F32) * above).astype(BF16)
        cat[a, TY : TY + CELLS, WIDE : 2 * WIDE] = src[a, 1 : TX + 1].reshape(CELLS, WIDE)
        cat[a, TY + CELLS :, WIDE : 2 * WIDE] = (src[a, TX + 1].astype(F32) * below).astype(BF16)

    def rows_of(a, dx):
        return cat[a, dx * TY : dx * TY + CELLS, :]

    def convolve(a, layer):
        return sum(dot(rows_of(a, dx), band[layer, dx], NT) for dx in range(3))

    sample = samples_ref[...]
    sample_cell = jnp.broadcast_to(lax.div(sample, NZ).astype(F32), (256, 256)).T
    sample_level = jnp.broadcast_to(lax.rem(sample, NZ).astype(F32), (256, 256)).T
    lane = iota((256, 256), 1)
    gather = jnp.where(sample_cell == lane.astype(F32), 1.0, 0.0).astype(BF16)
    level = jnp.where(sample_level == lax.div(lane, C).astype(F32), 1.0, 0.0)
    low_lanes = iota((64, 128), 1) < 64

    def gram(values):
        picked = dot(gather, values) * level
        full_gram = dot(picked.T.astype(BF16), picked.astype(BF16))
        even = full_gram[0:64, 0:128] + full_gram[128:192, 128:256]
        odd = full_gram[64:128, 0:128] + full_gram[192:256, 128:256]
        return even, odd

    count = float(n_gx * n_gy * 256)
    scale = 1.0 / jnp.sqrt(jnp.float32(n_gx * n_gy * CELLS * NZ))

    def two_grams(one, two):
        even, odd = gram(one)
        even2, odd2 = gram(two)
        both = jnp.where(low_lanes, even + swap_halves(odd), swap_halves(even2) + odd2)
        return (both / count).reshape(ring // 2, 128 // ring, 128)

    field = src[FIELD, 1 : TX + 1].reshape(CELLS, WIDE)
    cot = src[COT, 1 : TX + 1].reshape(CELLS, WIDE)
    gram_pay[: ring // 2] = two_grams(field, cot)

    chunk = HALF // ring

    def assemble(layer, flip):
        taps = [None] * 27
        for dx in range(3):
            for dy in range(3):

                def piece(a, h):
                    at = dy * WIDE + h * 128
                    return grads[layer, dx, a * 64 : (a + 1) * 64, at : at + 128]

                even, odd = piece(0, 0) + piece(2, 1), piece(1, 0) + piece(3, 1)
                pairs = ((odd, piece(2, 0)), (even, odd), (piece(1, 1), even))
                for e in range(3):
                    tap = (dx * 3 + dy) * 3 + e
                    taps[26 - tap if flip else tap] = pairs[e]
        for k in range(BLOCKS // 2):
            low, high = 2 * k, 2 * k + 1
            value = jnp.zeros((64, 128), F32)
            if low < 27:
                value = jnp.where(low_lanes, taps[low][0] + swap_halves(taps[low][1]), 0.0) * scale
            if high < 27:
                other = (swap_halves(taps[high][0]) + taps[high][1]) * scale
                value = jnp.where(low_lanes, value, other)
            per = chunk // 128
            half, rest = divmod(k, ring * per)
            at, p = divmod(rest, per)
            pay[layer, half, at, p * 64 : (p + 1) * 64, :] = value

    def send_on(layer):
        for k in ones[layer].order:
            from_core(layer, k).wait_recv()
            j = lax.rem(rank + k, ring)
            pay[layer, core, j] = pay[layer, core, j] + core_in[layer, j]
            ones[layer].outgoing(k).start()
        from_core(layer, 0).wait_recv()
        one_in[layer, rank] = pay[layer, core, rank] + core_in[layer, rank]

    frame(FIELD)
    hidden_pre = convolve(FIELD, 0)
    sigma = 1.0 / (1.0 + jnp.exp(-hidden_pre))
    hidden = (hidden_pre * sigma).astype(BF16)
    keep(HIDDEN, hidden)
    for d in range(8):
        halo(HIDDEN, d).start()

    frame(COT)
    hidden_t = hidden.astype(F32).T.astype(BF16)
    for dx in range(3):
        grads[1, dx] = dot(hidden_t, rows_of(COT, dx))
    assemble(1, True)
    for k in ones[1].order + [0]:
        to_core(1, k).start()

    back = jnp.zeros((CELLS, WIDE), F32)
    for dx in range(3):
        for dy in range(3):
            back += dot(
                cat[COT, dx * TY : dx * TY + CELLS, dy * WIDE : (dy + 1) * WIDE],
                band[1, 2 - dx, :, (2 - dy) * WIDE : (3 - dy) * WIDE],
            )
    delta = (back * sigma * (1.0 + hidden_pre * (1.0 - sigma))).astype(BF16)
    gram_pay[ring // 2 :] = two_grams(hidden, delta)
    gram_first.start()
    gram_one[y] = gram_pay[y]
    send_on(1)

    delta_t = delta.astype(F32).T.astype(BF16)
    for dx in range(3):
        grads[0, dx] = dot(delta_t, rows_of(FIELD, dx))
    assemble(0, False)
    for k in ones[0].order + [0]:
        to_core(0, k).start()
    send_on(0)

    gram_first.wait()
    gram_two[z] = jnp.sum(gram_one[...], axis=0)
    gram_second.start()

    frame(HIDDEN)
    output = (field.astype(F32) + convolve(HIDDEN, 1)).astype(BF16).astype(F32)
    for b in range(4):
        block = output[b * 64 : (b + 1) * 64]
        stacked = jnp.concatenate([block[:, j * 64 : (j + 1) * 64] for j in range(NZ)], axis=0)
        out_ref[b * 256 : (b + 1) * 256, :] = dot(to_cells, stacked.astype(BF16)).astype(BF16)
    store_out = pltpu.make_async_copy(out_ref, out_hbm, store_sem.at[0])
    store_out.start()

    gram_second.wait()
    gram_x[seat] = jnp.sum(gram_two[...], axis=0)
    gram_third.start()

    part = chunk // 2 // ring
    for layer in range(2):
        ones[layer].wait()
        total = one_in[layer, 0]
        for j in range(1, ring):
            total += one_in[layer, j]
        two_out[:, layer * part : (layer + 1) * part] = total.reshape(ring, part, 128)
    two_in[rank_two] = two_out[rank_two]
    two.start()
    for a in range(3):
        for d in range(8):
            halo(a, d).wait_send()

    gram_third.wait()
    gram_all[y] = jnp.sum(gram_x[...], axis=0)
    gram_gather.start()
    for k in range(ring):
        to_core(1, k).wait_send()
        to_core(0, k).wait_send()

    two.wait()
    x_in[x] = jnp.sum(two_in[...], axis=0)
    third.start()
    for stage in (ones[1], ones[0], gram_first):
        stage.settle()
    third.wait()
    whole[rank_two] = jnp.sum(x_in[...], axis=0)
    gather_two.start()

    gram_gather.wait()

    grams = gram_all[...].reshape(2, 64, 128)
    metric[...] = jnp.zeros((256, 256), F32)
    for m in range(4):
        lanes = slice((m // 2) * 128, (m // 2 + 1) * 128)
        mine = low_lanes if m % 2 == 0 else jnp.logical_not(low_lanes)
        block = grams[m // 2]
        metric[m * 64 : (m + 1) * 64, lanes] = jnp.where(mine, block, 0.0)
    eye = jnp.where(iota((256, 256), 0) == lane, 1.0, 0.0)
    matrix = metric[...] + 0.1 * eye
    norms = [
        jnp.sqrt(jnp.sum(matrix[m * 64 : (m + 1) * 64] * matrix[m * 64 : (m + 1) * 64]))
        for m in range(4)
    ]
    error = eye - jnp.concatenate(
        [matrix[m * 64 : (m + 1) * 64] / norms[m] for m in range(4)], axis=0
    )
    factor = eye + error
    parts = split(error)
    error = dot3(parts, parts)
    for step in range(1, NS_ITERS):
        parts = split(error)
        if step < NS_ITERS - 1:
            both = tuple(jnp.concatenate([f, e], axis=0) for f, e in zip(split(factor), parts))
            moved = dot3(both, parts)
            factor, error = factor + moved[0:256], moved[256:512]
        else:
            factor = factor + dot3(split(factor), parts)
    approx = jnp.concatenate([factor[m * 64 : (m + 1) * 64] / norms[m] for m in range(4)], axis=0)

    def twice(block, low):
        other = swap_halves(block)
        first, second = (block, other) if low else (other, block)
        return split(
            jnp.concatenate(
                [jnp.where(low_lanes, first, 0.0), jnp.where(low_lanes, 0.0, second)], axis=0
            )
        )

    left_first = twice(approx[0:64, 0:128], True)
    right_second = twice(approx[64:128, 0:128], False)
    none = jnp.zeros((64, 128), F32)
    left_second = split(
        jnp.concatenate([jnp.where(low_lanes, approx[128:192, 128:256], 0.0), none], axis=0)
    )
    right_first = split(
        jnp.where(low_lanes, swap_halves(approx[192:256, 128:256]), 0.0)
    )

    for stage in (two, third, gram_second, gram_third, gram_gather):
        stage.settle()
    gather_two.wait()
    pairs = chunk // 128
    both = [
        whole[:, layer * part : (layer + 1) * part].reshape(pairs, 64, 128) for layer in range(2)
    ]
    for p in range(pairs):
        block = split(jnp.concatenate([both[0][p], none], axis=0))
        result[core, rank, p, 0:64, :] = dot3(
            right_first, split(dot3(block, left_first))
        ).astype(BF16)
        block = split(jnp.concatenate([both[1][p], none], axis=0))
        done = dot3(split(dot3_t(right_second, block)), left_second)
        result[core, rank, p, 64:128, :] = jnp.where(
            low_lanes, done[0:64], swap_halves(done[64:128])
        ).astype(BF16)
    spread.start()
    to_back(0).start()
    for k in reversed(spread.order):
        spread.arrived(k)
        to_back(k).start()
    for k in [0] + spread.order[::-1]:
        from_back(k).wait_recv()

    for k in range(14):
        half, rest = divmod(k, HALF // 128)
        at, p = divmod(rest, pairs)
        lanes = 128 if k < 13 else 64
        first_out[:, k * 128 : k * 128 + lanes] = result[half, at, p, 0:64, 0:lanes]
        second_out[:, k * 128 : k * 128 + lanes] = result[half, at, p, 64:128, 0:lanes]

    for k in range(ring):
        to_back(k).wait_send()
    gather_two.settle()
    spread.settle()
    store_out.wait()


def solution(mesh):
    n_gx, n_gy = mesh.shape["gx"], mesh.shape["gy"]
    ring = n_gx // 4
    z_hi = ring // 2
    n_x = n_gy // z_hi
    chunk = HALF // ring
    most = max(ring, 2 * n_x)
    vmem = pl.BlockSpec(memory_space=pltpu.VMEM)
    anywhere = pl.BlockSpec(memory_space=pl.ANY)
    dma = pltpu.SemaphoreType.DMA

    def local(field, first_kernel, second_kernel, cotangent, samples):
        cells = field.shape[0] * field.shape[1] * field.shape[2]
        output, first, second = pl.pallas_call(
            functools.partial(kernel, (n_gx, n_gy, z_hi, ring, n_x)),
            out_shape=(
                jax.ShapeDtypeStruct((cells, C), BF16),
                jax.ShapeDtypeStruct((C, 27 * C), BF16),
                jax.ShapeDtypeStruct((C, 27 * C), BF16),
            ),
            in_specs=[anywhere] * 5,
            out_specs=(anywhere, vmem, vmem),
            scratch_shapes=[
                pltpu.VMEM((cells, C), BF16),
                pltpu.VMEM((C, 27 * C), BF16),
                pltpu.VMEM((C, 27 * C), BF16),
                pltpu.VMEM((cells, C), BF16),
                pltpu.VMEM((1, 256), jnp.int32),
                pltpu.VMEM((cells, C), BF16),
                pltpu.VMEM((3, TX + 8, TY, WIDE), BF16),
                pltpu.VMEM((3, 2, TX, WIDE), BF16),
                pltpu.VMEM((3, (TX + 2) * TY, 3 * WIDE), BF16),
                pltpu.VMEM((2, 3, WIDE, 3 * WIDE), BF16),
                pltpu.VMEM((2, 3, WIDE, 3 * WIDE), F32),
                pltpu.VMEM((2, 2, ring, chunk // 2, 128), F32),
                pltpu.VMEM((2, ring, chunk // 2, 128), F32),
                pltpu.VMEM((2, ring, chunk // 2, 128), F32),
                pltpu.VMEM((ring, chunk // ring, 128), F32),
                pltpu.VMEM((ring, chunk // ring, 128), F32),
                pltpu.VMEM((n_x, chunk // ring, 128), F32),
                pltpu.VMEM((ring, chunk // ring, 128), F32),
                pltpu.VMEM((2, ring, chunk // 128, 128, 128), BF16),
                pltpu.VMEM((ring, 128 // ring, 128), F32),
                pltpu.VMEM((ring, 128 // ring, 128), F32),
                pltpu.VMEM((ring, 128 // ring, 128), F32),
                pltpu.VMEM((2 * n_x, 128 // ring, 128), F32),
                pltpu.VMEM((ring, 128 // ring, 128), F32),
                pltpu.VMEM((256, 256), F32),
                dma((5,)),
                dma((1,)),
                dma((3, 8)),
                dma((3, 8)),
                dma((14, most)),
                dma((14, most)),
            ],
            compiler_params=pltpu.CompilerParams(
                collective_id=0, has_side_effects=True, vmem_limit_bytes=54 * 1024 * 1024
            ),
        )(
            field.reshape(cells, C),
            first_kernel.T,
            second_kernel.T,
            cotangent.reshape(cells, C),
            samples.reshape(1, -1),
        )
        return output.reshape(field.shape), first.astype(F32).T, second.astype(F32).T

    placed = (P("gx", "gy", None, None), P(), P(), P("gx", "gy", None, None), P("gx", "gy", None))
    return jax.shard_map(
        local,
        mesh=mesh,
        in_specs=placed,
        out_specs=(P("gx", "gy", None, None), P(), P()),
        check_vma=False,
    )
```

```python
import functools

import jax
import jax.numpy as jnp
from jax import lax
from jax.experimental import pallas as pl
from jax.experimental.pallas import tpu as pltpu
from jax.sharding import PartitionSpec as P

MESH = pl.DeviceIdType.MESH
F32 = jnp.float32
BF16 = jnp.bfloat16
NS_ITERS = 5
C = 64
TX = 16
TY = 16
NZ = 4
WIDE = NZ * C
CELLS = TX * TY
BLOCKS = 32
HALF = BLOCKS * 64 // 2
FIELD, COT, HIDDEN = 0, 1, 2
NN = (((1,), (0,)), ((), ()))
NT = (((1,), (1,)), ((), ()))


def dot(a, b, dims=NN):
    return lax.dot_general(a, b, dims, preferred_element_type=F32)


def split(value):
    high = value.astype(BF16)
    return high, (value - high.astype(F32)).astype(BF16)


def dot3(a, b):
    return dot(jnp.concatenate([a[0], a[0], a[1]], axis=1), jnp.concatenate([b[0], b[1], b[0]], axis=0))


def dot3_t(a, b):
    return dot(
        jnp.concatenate([a[0], a[0], a[1]], axis=1), jnp.concatenate([b[0], b[1], b[0]], axis=1), NT
    )


def iota(shape, dim):
    return lax.broadcasted_iota(jnp.int32, shape, dim)


def onehot(target, shape):
    return jnp.where(iota(shape, 1) == target, 1.0, 0.0).astype(BF16)


def swap_halves(value):
    return pltpu.roll(value, 64, 1)


def by_distance(count):
    return sorted(range(1, count), key=lambda k: -min(k, count - k))


def kernel(
    sizes,
    field_hbm,
    first_hbm,
    second_hbm,
    cot_hbm,
    samples_hbm,
    out_hbm,
    first_out,
    second_out,
    field_ref,
    first_ref,
    second_ref,
    cot_ref,
    samples_ref,
    out_ref,
    src,
    col,
    cat,
    band,
    grads,
    pay,
    core_in,
    one_in,
    two_out,
    two_in,
    x_in,
    whole,
    result,
    gram_pay,
    gram_one,
    gram_two,
    gram_x,
    gram_all,
    metric,
    load_sem,
    store_sem,
    halo_send,
    halo_recv,
    send_sems,
    recv_sems,
):
    n_gx, n_gy, z_hi, ring, n_x = sizes
    gx = lax.axis_index("gx")
    gy = lax.axis_index("gy")
    core = lax.rem(gx, 2)
    z_low = lax.rem(lax.div(gx, 2), 2)
    y = lax.div(gx, 4)
    x = lax.div(gy, z_hi)
    z = lax.rem(gy, z_hi) * 2 + z_low

    def load(k, source, target):
        return pltpu.make_async_copy(source, target, load_sem.at[k])

    loads = [
        load(k, *pair)
        for k, pair in enumerate(
            (
                (field_hbm, field_ref),
                (cot_hbm, cot_ref),
                (first_hbm, first_ref),
                (second_hbm, second_ref),
                (samples_hbm, samples_ref),
            )
        )
    ]
    for one in loads:
        one.start()

    rank = y + core * (z - y)
    rank_two = z + core * (y - z)
    partner = (gx + 1 - 2 * core, gy)

    def along_y(j):
        return gx + 4 * (j - y), gy

    def along_z(j):
        return gx + 2 * (lax.rem(j, 2) - z_low), x * z_hi + lax.div(j, 2)

    def on_ring(j):
        (ax, ay), (bx, by) = along_y(j), along_z(j)
        return (ax + core * (bx - ax), ay + core * (by - ay))

    def on_ring_two(j):
        (bx, by), (ax, ay) = along_y(j), along_z(j)
        return (ax + core * (bx - ax), ay + core * (by - ay))

    def along_x(j):
        return (gx, gy + z_hi * (j - x))

    seat = x * 2 + core

    def along_seats(j):
        return (gx + lax.rem(j, 2) - core, gy + z_hi * (lax.div(j, 2) - x))

    def neighbour(dx, dy):
        return (lax.rem(gx + n_gx + dx, n_gx), lax.rem(gy + n_gy + dy, n_gy))

    barrier = pltpu.get_barrier_semaphore()

    def signal(where):
        pl.semaphore_signal(barrier, inc=1, device_id=where, device_id_type=MESH)

    sides = ((1, 0), (-1, 0), (0, 1), (0, -1), (1, 1), (1, -1), (-1, 1), (-1, -1))
    for side in sides:
        signal(neighbour(*side))
    for k in by_distance(ring):
        signal(on_ring(lax.rem(rank + k, ring)))
        signal(on_ring_two(lax.rem(rank_two + k, ring)))
    for k in range(1, 2 * n_x):
        signal(along_seats(lax.rem(seat + k, 2 * n_x)))

    def copy(source, target, send, recv, where):
        return pltpu.make_async_remote_copy(
            src_ref=source,
            dst_ref=target,
            send_sem=send,
            recv_sem=recv,
            device_id=where,
            device_id_type=MESH,
        )

    def halo(a, d):
        side = sides[d]
        if side[0] == 0:
            source = col.at[a, 1 if side[1] > 0 else 0]
        else:
            source = src.at[a, TX if side[0] > 0 else 1]
        landing = (0, TX + 1, TX + 2, TX + 3, TX + 4, TX + 5, TX + 6, TX + 7)[d]
        return copy(
            source, src.at[a, landing], halo_send.at[a, d], halo_recv.at[a, d], neighbour(*side)
        )

    class Exchange:
        def __init__(self, stage, count, me, where, source, target):
            self.stage, self.count, self.me, self.where = stage, count, me, where
            self.source, self.target = source, target
            self.order = by_distance(count)

        def outgoing(self, k):
            j = lax.rem(self.me + k, self.count)
            return copy(
                self.source(j),
                self.target(self.me),
                send_sems.at[self.stage, k],
                recv_sems.at[self.stage, k],
                self.where(j),
            )

        def sender(self, k):
            return lax.rem(self.me + self.count - k, self.count)

        def start(self):
            for k in self.order:
                self.outgoing(k).start()

        def arrived(self, k):
            there = self.target(self.sender(k))
            copy(
                there, there, send_sems.at[self.stage, k], recv_sems.at[self.stage, k], partner
            ).wait_recv()

        def wait(self):
            for k in reversed(self.order):
                self.arrived(k)

        def settle(self):
            for k in self.order:
                self.outgoing(k).wait_send()

    def to_core(layer, k):
        j = lax.rem(rank_two + k, ring)
        return copy(
            pay.at[layer, 1 - core, j],
            core_in.at[layer, j],
            send_sems.at[12 * layer, k],
            recv_sems.at[12 * layer, k],
            partner,
        )

    def from_core(layer, k):
        j = lax.rem(rank + k, ring)
        return copy(
            pay.at[layer, core, j],
            core_in.at[layer, j],
            send_sems.at[12 * layer, k],
            recv_sems.at[12 * layer, k],
            partner,
        )

    def to_back(k):
        there = result.at[core, lax.rem(rank + ring - k, ring)]
        return copy(there, there, send_sems.at[1, k], recv_sems.at[1, k], partner)

    def from_back(k):
        there = result.at[1 - core, lax.rem(rank_two + ring - k, ring)]
        return copy(there, there, send_sems.at[1, k], recv_sems.at[1, k], partner)

    ones = [
        Exchange(
            stage,
            ring,
            rank,
            on_ring,
            functools.partial(lambda layer, j: pay.at[layer, core, j], layer),
            functools.partial(lambda layer, j: one_in.at[layer, j], layer),
        )
        for layer, stage in enumerate((2, 13))
    ]
    two = Exchange(3, ring, rank_two, on_ring_two, lambda j: two_out.at[j], lambda j: two_in.at[j])
    third = Exchange(4, n_x, x, along_x, lambda j: x_in.at[x], lambda j: x_in.at[j])
    gather_two = Exchange(
        5, ring, rank_two, on_ring_two, lambda j: whole.at[rank_two], lambda j: whole.at[j]
    )
    spread = Exchange(
        6, ring, rank, on_ring, lambda j: result.at[core, rank], lambda j: result.at[core, j]
    )
    gram_first = Exchange(
        8, ring, y, along_y, lambda j: gram_pay.at[j], lambda j: gram_one.at[j]
    )
    gram_second = Exchange(
        9, ring, z, along_z, lambda j: gram_two.at[z], lambda j: gram_two.at[j]
    )
    gram_third = Exchange(
        10, 2 * n_x, seat, along_seats, lambda j: gram_x.at[seat], lambda j: gram_x.at[j]
    )
    gram_gather = Exchange(
        11, ring, y, along_y, lambda j: gram_all.at[y], lambda j: gram_all.at[j]
    )

    edge_rows = iota((2 * TX, 1), 0)
    edges = onehot(jnp.where(edge_rows < TX, edge_rows * TY, (edge_rows - TX) * TY + TY - 1), (2 * TX, CELLS))

    def keep(a, value):
        src[a, 1 : TX + 1] = value.reshape(TX, TY, WIDE)
        col[a] = dot(edges, value).astype(BF16).reshape(2, TX, WIDE)

    rows256 = iota((256, 1), 0)
    to_columns = onehot(lax.rem(rows256, 64) * NZ + lax.div(rows256, 64), (256, 256))
    to_cells = onehot(lax.rem(rows256, NZ) * 64 + lax.div(rows256, NZ), (256, 256))

    def columns_of(ref):
        out = []
        for b in range(4):
            moved = dot(to_columns, ref[b * 256 : (b + 1) * 256, :])
            out.append(jnp.concatenate([moved[i * 64 : (i + 1) * 64] for i in range(NZ)], axis=1))
        return jnp.concatenate(out, axis=0).astype(BF16)

    loads[0].wait()
    keep(FIELD, columns_of(field_ref))
    loads[1].wait()
    keep(COT, columns_of(cot_ref))
    pl.semaphore_wait(barrier, len(sides) + 2 * (ring - 1) + 2 * n_x - 1)
    for d in range(8):
        halo(FIELD, d).start()
    for d in range(8):
        halo(COT, d).start()

    def build_band(layer, ref):
        nothing = jnp.zeros((64, 64), F32)
        for k in range(9):
            low, mid, high = (
                ref[:, (3 * k + i) * 64 : (3 * k + i + 1) * 64].astype(F32) for i in range(3)
            )
            lanes = slice((k % 3) * WIDE, (k % 3 + 1) * WIDE)
            for out_z, parts in enumerate(
                (
                    (mid, high, nothing, nothing),
                    (low, mid, high, nothing),
                    (nothing, low, mid, high),
                    (nothing, nothing, low, mid),
                )
            ):
                band[layer, k // 3, out_z * 64 : (out_z + 1) * 64, lanes] = jnp.concatenate(
                    parts, axis=1
                ).astype(BF16)

    loads[2].wait()
    build_band(0, first_ref)
    loads[3].wait()
    build_band(1, second_ref)
    loads[4].wait()
    framed_rows = (TX + 2) * TY
    source_rows = (TX + 8) * TY
    i = iota((framed_rows, 1), 0)
    r = lax.div(i, TY)
    c = lax.rem(i, TY)
    first_row, last_row = jnp.where(gx == 0, 0, -1), jnp.where(gx == n_gx - 1, TX + 1, -1)
    first_col, last_col = jnp.where(gy == 0, 0, -1), jnp.where(gy == n_gy - 1, TY - 1, -1)
    outside = (r == first_row) | (r == last_row)

    def shifted(step, at, column_slot, low_slot, high_slot, pick, outer):
        edge = jnp.where(
            r == 0,
            low_slot * TY + pick,
            jnp.where(r == TX + 1, high_slot * TY + pick, column_slot * TY + r - 1),
        )
        target = jnp.where(c == at, edge, i + step)
        return onehot(jnp.where(outside | (c == outer), -1, target), (framed_rows, source_rows))

    shift_low = shifted(-1, 0, TX + 2, TX + 4, TX + 6, TY - 1, first_col)
    shift_high = shifted(1, TY - 1, TX + 3, TX + 5, TX + 7, 0, last_col)
    above = jnp.where(gx == 0, 0.0, 1.0)
    below = jnp.where(gx == n_gx - 1, 0.0, 1.0)

    def frame(a):
        for d in range(8):
            halo(a, d).wait_recv()
        whole = src[a].reshape(source_rows, WIDE)
        cat[a, :, 0:WIDE] = dot(shift_low, whole).astype(BF16)
        cat[a, :, 2 * WIDE : 3 * WIDE] = dot(shift_high, whole).astype(BF16)
        cat[a, 0:TY, WIDE : 2 * WIDE] = (src[a, 0].astype(F32) * above).astype(BF16)
        cat[a, TY : TY + CELLS, WIDE : 2 * WIDE] = src[a, 1 : TX + 1].reshape(CELLS, WIDE)
        cat[a, TY + CELLS :, WIDE : 2 * WIDE] = (src[a, TX + 1].astype(F32) * below).astype(BF16)

    def rows_of(a, dx):
        return cat[a, dx * TY : dx * TY + CELLS, :]

    def convolve(a, layer):
        return sum(dot(rows_of(a, dx), band[layer, dx], NT) for dx in range(3))

    sample = samples_ref[...]
    sample_cell = jnp.broadcast_to(lax.div(sample, NZ).astype(F32), (256, 256)).T
    sample_level = jnp.broadcast_to(lax.rem(sample, NZ).astype(F32), (256, 256)).T
    lane = iota((256, 256), 1)
    gather = jnp.where(sample_cell == lane.astype(F32), 1.0, 0.0).astype(BF16)
    level = jnp.where(sample_level == lax.div(lane, C).astype(F32), 1.0, 0.0)
    low_lanes = iota((64, 128), 1) < 64

    def gram(values):
        picked = dot(gather, values) * level
        full_gram = dot(picked.T.astype(BF16), picked.astype(BF16))
        even = full_gram[0:64, 0:128] + full_gram[128:192, 128:256]
        odd = full_gram[64:128, 0:128] + full_gram[192:256, 128:256]
        return even, odd

    count = float(n_gx * n_gy * 256)
    scale = 1.0 / jnp.sqrt(jnp.float32(n_gx * n_gy * CELLS * NZ))

    def two_grams(one, two):
        even, odd = gram(one)
        even2, odd2 = gram(two)
        both = jnp.where(low_lanes, even + swap_halves(odd), swap_halves(even2) + odd2)
        return (both / count).reshape(ring // 2, 128 // ring, 128)

    field = src[FIELD, 1 : TX + 1].reshape(CELLS, WIDE)
    cot = src[COT, 1 : TX + 1].reshape(CELLS, WIDE)
    gram_pay[: ring // 2] = two_grams(field, cot)

    chunk = HALF // ring

    def assemble(layer, flip):
        taps = [None] * 27
        for dx in range(3):
            for dy in range(3):

                def piece(a, h):
                    at = dy * WIDE + h * 128
                    return grads[layer, dx, a * 64 : (a + 1) * 64, at : at + 128]

                even, odd = piece(0, 0) + piece(2, 1), piece(1, 0) + piece(3, 1)
                pairs = ((odd, piece(2, 0)), (even, odd), (piece(1, 1), even))
                for e in range(3):
                    tap = (dx * 3 + dy) * 3 + e
                    taps[26 - tap if flip else tap] = pairs[e]
        for k in range(BLOCKS // 2):
            low, high = 2 * k, 2 * k + 1
            value = jnp.zeros((64, 128), F32)
            if low < 27:
                value = jnp.where(low_lanes, taps[low][0] + swap_halves(taps[low][1]), 0.0) * scale
            if high < 27:
                other = (swap_halves(taps[high][0]) + taps[high][1]) * scale
                value = jnp.where(low_lanes, value, other)
            per = chunk // 128
            half, rest = divmod(k, ring * per)
            at, p = divmod(rest, per)
            pay[layer, half, at, p * 64 : (p + 1) * 64, :] = value

    def send_on(layer):
        for k in ones[layer].order:
            from_core(layer, k).wait_recv()
            j = lax.rem(rank + k, ring)
            pay[layer, core, j] = pay[layer, core, j] + core_in[layer, j]
            ones[layer].outgoing(k).start()
        from_core(layer, 0).wait_recv()
        one_in[layer, rank] = pay[layer, core, rank] + core_in[layer, rank]

    frame(FIELD)
    hidden_pre = convolve(FIELD, 0)
    sigma = 1.0 / (1.0 + jnp.exp(-hidden_pre))
    hidden = (hidden_pre * sigma).astype(BF16)
    keep(HIDDEN, hidden)
    for d in range(8):
        halo(HIDDEN, d).start()

    frame(COT)
    hidden_t = hidden.astype(F32).T.astype(BF16)
    for dx in range(3):
        grads[1, dx] = dot(hidden_t, rows_of(COT, dx))
    assemble(1, True)
    for k in ones[1].order + [0]:
        to_core(1, k).start()

    back = jnp.zeros((CELLS, WIDE), F32)
    for dx in range(3):
        for dy in range(3):
            back += dot(
                cat[COT, dx * TY : dx * TY + CELLS, dy * WIDE : (dy + 1) * WIDE],
                band[1, 2 - dx, :, (2 - dy) * WIDE : (3 - dy) * WIDE],
            )
    delta = (back * sigma * (1.0 + hidden_pre * (1.0 - sigma))).astype(BF16)
    gram_pay[ring // 2 :] = two_grams(hidden, delta)
    gram_first.start()
    gram_one[y] = gram_pay[y]
    send_on(1)

    delta_t = delta.astype(F32).T.astype(BF16)
    for dx in range(3):
        grads[0, dx] = dot(delta_t, rows_of(FIELD, dx))
    assemble(0, False)
    for k in ones[0].order + [0]:
        to_core(0, k).start()
    send_on(0)

    gram_first.wait()
    gram_two[z] = jnp.sum(gram_one[...], axis=0)
    gram_second.start()

    frame(HIDDEN)
    output = (field.astype(F32) + convolve(HIDDEN, 1)).astype(BF16).astype(F32)
    for b in range(4):
        block = output[b * 64 : (b + 1) * 64]
        stacked = jnp.concatenate([block[:, j * 64 : (j + 1) * 64] for j in range(NZ)], axis=0)
        out_ref[b * 256 : (b + 1) * 256, :] = dot(to_cells, stacked.astype(BF16)).astype(BF16)
    store_out = pltpu.make_async_copy(out_ref, out_hbm, store_sem.at[0])
    store_out.start()

    gram_second.wait()
    gram_x[seat] = jnp.sum(gram_two[...], axis=0)
    gram_third.start()

    part = chunk // 2 // ring
    for layer in range(2):
        ones[layer].wait()
        total = one_in[layer, 0]
        for j in range(1, ring):
            total += one_in[layer, j]
        two_out[:, layer * part : (layer + 1) * part] = total.reshape(ring, part, 128)
    two_in[rank_two] = two_out[rank_two]
    two.start()
    for a in range(3):
        for d in range(8):
            halo(a, d).wait_send()

    gram_third.wait()
    gram_all[y] = jnp.sum(gram_x[...], axis=0)
    gram_gather.start()
    for k in range(ring):
        to_core(1, k).wait_send()
        to_core(0, k).wait_send()

    two.wait()
    x_in[x] = jnp.sum(two_in[...], axis=0)
    third.start()
    for stage in (ones[1], ones[0], gram_first):
        stage.settle()
    third.wait()
    whole[rank_two] = jnp.sum(x_in[...], axis=0)
    gather_two.start()

    gram_gather.wait()

    grams = gram_all[...].reshape(2, 64, 128)
    metric[...] = jnp.zeros((256, 256), F32)
    for m in range(4):
        lanes = slice((m // 2) * 128, (m // 2 + 1) * 128)
        mine = low_lanes if m % 2 == 0 else jnp.logical_not(low_lanes)
        block = grams[m // 2]
        metric[m * 64 : (m + 1) * 64, lanes] = jnp.where(mine, block, 0.0)
    eye = jnp.where(iota((256, 256), 0) == lane, 1.0, 0.0)
    matrix = metric[...] + 0.1 * eye
    norms = [
        jnp.sqrt(jnp.sum(matrix[m * 64 : (m + 1) * 64] * matrix[m * 64 : (m + 1) * 64]))
        for m in range(4)
    ]
    error = eye - jnp.concatenate(
        [matrix[m * 64 : (m + 1) * 64] / norms[m] for m in range(4)], axis=0
    )
    factor = eye + error
    parts = split(error)
    error = dot3(parts, parts)
    for step in range(1, NS_ITERS):
        parts = split(error)
        if step < NS_ITERS - 1:
            both = tuple(jnp.concatenate([f, e], axis=0) for f, e in zip(split(factor), parts))
            moved = dot3(both, parts)
            factor, error = factor + moved[0:256], moved[256:512]
        else:
            factor = factor + dot3(split(factor), parts)
    approx = jnp.concatenate([factor[m * 64 : (m + 1) * 64] / norms[m] for m in range(4)], axis=0)

    def twice(block, low):
        other = swap_halves(block)
        first, second = (block, other) if low else (other, block)
        return split(
            jnp.concatenate(
                [jnp.where(low_lanes, first, 0.0), jnp.where(low_lanes, 0.0, second)], axis=0
            )
        )

    left_first = twice(approx[0:64, 0:128], True)
    right_second = twice(approx[64:128, 0:128], False)
    none = jnp.zeros((64, 128), F32)
    left_second = split(
        jnp.concatenate([jnp.where(low_lanes, approx[128:192, 128:256], 0.0), none], axis=0)
    )
    right_first = split(
        jnp.where(low_lanes, swap_halves(approx[192:256, 128:256]), 0.0)
    )

    for stage in (two, third, gram_second, gram_third, gram_gather):
        stage.settle()
    gather_two.wait()
    pairs = chunk // 128
    both = [
        whole[:, layer * part : (layer + 1) * part].reshape(pairs, 64, 128) for layer in range(2)
    ]
    for p in range(pairs):
        block = split(jnp.concatenate([both[0][p], none], axis=0))
        result[core, rank, p, 0:64, :] = dot3(
            right_first, split(dot3(block, left_first))
        ).astype(BF16)
        block = split(jnp.concatenate([both[1][p], none], axis=0))
        done = dot3(split(dot3_t(right_second, block)), left_second)
        result[core, rank, p, 64:128, :] = jnp.where(
            low_lanes, done[0:64], swap_halves(done[64:128])
        ).astype(BF16)
    spread.start()
    to_back(0).start()
    for k in reversed(spread.order):
        spread.arrived(k)
        to_back(k).start()
    for k in [0] + spread.order[::-1]:
        from_back(k).wait_recv()

    for k in range(14):
        half, rest = divmod(k, HALF // 128)
        at, p = divmod(rest, pairs)
        lanes = 128 if k < 13 else 64
        first_out[:, k * 128 : k * 128 + lanes] = result[half, at, p, 0:64, 0:lanes]
        second_out[:, k * 128 : k * 128 + lanes] = result[half, at, p, 64:128, 0:lanes]

    for k in range(ring):
        to_back(k).wait_send()
    gather_two.settle()
    spread.settle()
    store_out.wait()


def solution(mesh):
    n_gx, n_gy = mesh.shape["gx"], mesh.shape["gy"]
    ring = n_gx // 4
    z_hi = ring // 2
    n_x = n_gy // z_hi
    chunk = HALF // ring
    most = max(ring, 2 * n_x)
    vmem = pl.BlockSpec(memory_space=pltpu.VMEM)
    anywhere = pl.BlockSpec(memory_space=pl.ANY)
    dma = pltpu.SemaphoreType.DMA

    def local(field, first_kernel, second_kernel, cotangent, samples):
        cells = field.shape[0] * field.shape[1] * field.shape[2]
        output, first, second = pl.pallas_call(
            functools.partial(kernel, (n_gx, n_gy, z_hi, ring, n_x)),
            out_shape=(
                jax.ShapeDtypeStruct((cells, C), BF16),
                jax.ShapeDtypeStruct((C, 27 * C), BF16),
                jax.ShapeDtypeStruct((C, 27 * C), BF16),
            ),
            in_specs=[anywhere] * 5,
            out_specs=(anywhere, vmem, vmem),
            scratch_shapes=[
                pltpu.VMEM((cells, C), BF16),
                pltpu.VMEM((C, 27 * C), BF16),
                pltpu.VMEM((C, 27 * C), BF16),
                pltpu.VMEM((cells, C), BF16),
                pltpu.VMEM((1, 256), jnp.int32),
                pltpu.VMEM((cells, C), BF16),
                pltpu.VMEM((3, TX + 8, TY, WIDE), BF16),
                pltpu.VMEM((3, 2, TX, WIDE), BF16),
                pltpu.VMEM((3, (TX + 2) * TY, 3 * WIDE), BF16),
                pltpu.VMEM((2, 3, WIDE, 3 * WIDE), BF16),
                pltpu.VMEM((2, 3, WIDE, 3 * WIDE), F32),
                pltpu.VMEM((2, 2, ring, chunk // 2, 128), F32),
                pltpu.VMEM((2, ring, chunk // 2, 128), F32),
                pltpu.VMEM((2, ring, chunk // 2, 128), F32),
                pltpu.VMEM((ring, chunk // ring, 128), F32),
                pltpu.VMEM((ring, chunk // ring, 128), F32),
                pltpu.VMEM((n_x, chunk // ring, 128), F32),
                pltpu.VMEM((ring, chunk // ring, 128), F32),
                pltpu.VMEM((2, ring, chunk // 128, 128, 128), BF16),
                pltpu.VMEM((ring, 128 // ring, 128), F32),
                pltpu.VMEM((ring, 128 // ring, 128), F32),
                pltpu.VMEM((ring, 128 // ring, 128), F32),
                pltpu.VMEM((2 * n_x, 128 // ring, 128), F32),
                pltpu.VMEM((ring, 128 // ring, 128), F32),
                pltpu.VMEM((256, 256), F32),
                dma((5,)),
                dma((1,)),
                dma((3, 8)),
                dma((3, 8)),
                dma((14, most)),
                dma((14, most)),
            ],
            compiler_params=pltpu.CompilerParams(
                collective_id=0, has_side_effects=True, vmem_limit_bytes=(53 * 1024 + 360) * 1024
            ),
        )(
            field.reshape(cells, C),
            first_kernel.T,
            second_kernel.T,
            cotangent.reshape(cells, C),
            samples.reshape(1, -1),
        )
        return output.reshape(field.shape), first.astype(F32).T, second.astype(F32).T

    placed = (P("gx", "gy", None, None), P(), P(), P("gx", "gy", None, None), P("gx", "gy", None))
    return jax.shard_map(
        local,
        mesh=mesh,
        in_specs=placed,
        out_specs=(P("gx", "gy", None, None), P(), P()),
        check_vma=False,
    )
```

```python
import functools

import jax
import jax.numpy as jnp
from jax import lax
from jax.experimental import pallas as pl
from jax.experimental.pallas import tpu as pltpu
from jax.sharding import PartitionSpec as P

MESH = pl.DeviceIdType.MESH
F32 = jnp.float32
BF16 = jnp.bfloat16
NS_ITERS = 5
C = 64
TX = 16
TY = 16
NZ = 4
WIDE = NZ * C
CELLS = TX * TY
BLOCKS = 32
HALF = BLOCKS * 64 // 2
FIELD, COT, HIDDEN = 0, 1, 2
NN = (((1,), (0,)), ((), ()))
NT = (((1,), (1,)), ((), ()))


def dot(a, b, dims=NN):
    return lax.dot_general(a, b, dims, preferred_element_type=F32)


def split(value):
    high = value.astype(BF16)
    return high, (value - high.astype(F32)).astype(BF16)


def dot3(a, b):
    return dot(jnp.concatenate([a[0], a[0], a[1]], axis=1), jnp.concatenate([b[0], b[1], b[0]], axis=0))


def dot3_t(a, b):
    return dot(
        jnp.concatenate([a[0], a[0], a[1]], axis=1), jnp.concatenate([b[0], b[1], b[0]], axis=1), NT
    )


def iota(shape, dim):
    return lax.broadcasted_iota(jnp.int32, shape, dim)


def onehot(target, shape):
    return jnp.where(iota(shape, 1) == target, 1.0, 0.0).astype(BF16)


def swap_halves(value):
    return pltpu.roll(value, 64, 1)


def by_distance(count):
    return sorted(range(1, count), key=lambda k: -min(k, count - k))


def kernel(
    sizes,
    field_hbm,
    first_hbm,
    second_hbm,
    cot_hbm,
    samples_hbm,
    out_hbm,
    first_out,
    second_out,
    field_ref,
    first_ref,
    second_ref,
    cot_ref,
    samples_ref,
    out_ref,
    src,
    col,
    cat,
    band,
    grads,
    pay,
    core_in,
    one_in,
    two_out,
    two_in,
    x_in,
    whole,
    result,
    gram_pay,
    gram_one,
    gram_two,
    gram_x,
    gram_all,
    metric,
    load_sem,
    store_sem,
    halo_send,
    halo_recv,
    send_sems,
    recv_sems,
):
    n_gx, n_gy, z_hi, ring, n_x = sizes
    gx = lax.axis_index("gx")
    gy = lax.axis_index("gy")
    core = lax.rem(gx, 2)
    z_low = lax.rem(lax.div(gx, 2), 2)
    y = lax.div(gx, 4)
    x = lax.div(gy, z_hi)
    z = lax.rem(gy, z_hi) * 2 + z_low

    def load(k, source, target):
        return pltpu.make_async_copy(source, target, load_sem.at[k])

    loads = [
        load(k, *pair)
        for k, pair in enumerate(
            (
                (field_hbm, field_ref),
                (cot_hbm, cot_ref),
                (first_hbm, first_ref),
                (second_hbm, second_ref),
                (samples_hbm, samples_ref),
            )
        )
    ]
    for one in loads:
        one.start()

    rank = y + core * (z - y)
    rank_two = z + core * (y - z)
    partner = (gx + 1 - 2 * core, gy)

    def along_y(j):
        return gx + 4 * (j - y), gy

    def along_z(j):
        return gx + 2 * (lax.rem(j, 2) - z_low), x * z_hi + lax.div(j, 2)

    def on_ring(j):
        (ax, ay), (bx, by) = along_y(j), along_z(j)
        return (ax + core * (bx - ax), ay + core * (by - ay))

    def on_ring_two(j):
        (bx, by), (ax, ay) = along_y(j), along_z(j)
        return (ax + core * (bx - ax), ay + core * (by - ay))

    def along_x(j):
        return (gx, gy + z_hi * (j - x))

    seat = x * 2 + core

    def along_seats(j):
        return (gx + lax.rem(j, 2) - core, gy + z_hi * (lax.div(j, 2) - x))

    def neighbour(dx, dy):
        return (lax.rem(gx + n_gx + dx, n_gx), lax.rem(gy + n_gy + dy, n_gy))

    barrier = pltpu.get_barrier_semaphore()

    def signal(where):
        pl.semaphore_signal(barrier, inc=1, device_id=where, device_id_type=MESH)

    sides = ((1, 0), (-1, 0), (0, 1), (0, -1), (1, 1), (1, -1), (-1, 1), (-1, -1))
    for side in sides:
        signal(neighbour(*side))
    for k in by_distance(ring):
        signal(on_ring(lax.rem(rank + k, ring)))
        signal(on_ring_two(lax.rem(rank_two + k, ring)))
    for k in range(1, 2 * n_x):
        signal(along_seats(lax.rem(seat + k, 2 * n_x)))

    def copy(source, target, send, recv, where):
        return pltpu.make_async_remote_copy(
            src_ref=source,
            dst_ref=target,
            send_sem=send,
            recv_sem=recv,
            device_id=where,
            device_id_type=MESH,
        )

    def halo(a, d):
        side = sides[d]
        if side[0] == 0:
            source = col.at[a, 1 if side[1] > 0 else 0]
        else:
            source = src.at[a, TX if side[0] > 0 else 1]
        landing = (0, TX + 1, TX + 2, TX + 3, TX + 4, TX + 5, TX + 6, TX + 7)[d]
        return copy(
            source, src.at[a, landing], halo_send.at[a, d], halo_recv.at[a, d], neighbour(*side)
        )

    class Exchange:
        def __init__(self, stage, count, me, where, source, target):
            self.stage, self.count, self.me, self.where = stage, count, me, where
            self.source, self.target = source, target
            self.order = by_distance(count)

        def outgoing(self, k):
            j = lax.rem(self.me + k, self.count)
            return copy(
                self.source(j),
                self.target(self.me),
                send_sems.at[self.stage, k],
                recv_sems.at[self.stage, k],
                self.where(j),
            )

        def sender(self, k):
            return lax.rem(self.me + self.count - k, self.count)

        def start(self):
            for k in self.order:
                self.outgoing(k).start()

        def arrived(self, k):
            there = self.target(self.sender(k))
            copy(
                there, there, send_sems.at[self.stage, k], recv_sems.at[self.stage, k], partner
            ).wait_recv()

        def wait(self):
            for k in reversed(self.order):
                self.arrived(k)

        def settle(self):
            for k in self.order:
                self.outgoing(k).wait_send()

    def to_core(layer, k):
        j = lax.rem(rank_two + k, ring)
        return copy(
            pay.at[layer, 1 - core, j],
            core_in.at[layer, j],
            send_sems.at[12 * layer, k],
            recv_sems.at[12 * layer, k],
            partner,
        )

    def from_core(layer, k):
        j = lax.rem(rank + k, ring)
        return copy(
            pay.at[layer, core, j],
            core_in.at[layer, j],
            send_sems.at[12 * layer, k],
            recv_sems.at[12 * layer, k],
            partner,
        )

    def to_back(k):
        there = result.at[core, lax.rem(rank + ring - k, ring)]
        return copy(there, there, send_sems.at[1, k], recv_sems.at[1, k], partner)

    def from_back(k):
        there = result.at[1 - core, lax.rem(rank_two + ring - k, ring)]
        return copy(there, there, send_sems.at[1, k], recv_sems.at[1, k], partner)

    ones = [
        Exchange(
            stage,
            ring,
            rank,
            on_ring,
            functools.partial(lambda layer, j: pay.at[layer, core, j], layer),
            functools.partial(lambda layer, j: one_in.at[layer, j], layer),
        )
        for layer, stage in enumerate((2, 13))
    ]
    two = Exchange(3, ring, rank_two, on_ring_two, lambda j: two_out.at[j], lambda j: two_in.at[j])
    third = Exchange(4, n_x, x, along_x, lambda j: x_in.at[x], lambda j: x_in.at[j])
    gather_two = Exchange(
        5, ring, rank_two, on_ring_two, lambda j: whole.at[rank_two], lambda j: whole.at[j]
    )
    spread = Exchange(
        6, ring, rank, on_ring, lambda j: result.at[core, rank], lambda j: result.at[core, j]
    )
    gram_first = Exchange(
        8, ring, y, along_y, lambda j: gram_pay.at[j], lambda j: gram_one.at[j]
    )
    gram_second = Exchange(
        9, ring, z, along_z, lambda j: gram_two.at[z], lambda j: gram_two.at[j]
    )
    gram_third = Exchange(
        10, 2 * n_x, seat, along_seats, lambda j: gram_x.at[seat], lambda j: gram_x.at[j]
    )
    gram_gather = Exchange(
        11, ring, y, along_y, lambda j: gram_all.at[y], lambda j: gram_all.at[j]
    )

    edge_rows = iota((2 * TX, 1), 0)
    edges = onehot(jnp.where(edge_rows < TX, edge_rows * TY, (edge_rows - TX) * TY + TY - 1), (2 * TX, CELLS))

    def keep(a, value):
        src[a, 1 : TX + 1] = value.reshape(TX, TY, WIDE)
        col[a] = dot(edges, value).astype(BF16).reshape(2, TX, WIDE)

    rows256 = iota((256, 1), 0)
    to_columns = onehot(lax.rem(rows256, 64) * NZ + lax.div(rows256, 64), (256, 256))
    to_cells = onehot(lax.rem(rows256, NZ) * 64 + lax.div(rows256, NZ), (256, 256))

    def columns_of(ref):
        out = []
        for b in range(4):
            moved = dot(to_columns, ref[b * 256 : (b + 1) * 256, :])
            out.append(jnp.concatenate([moved[i * 64 : (i + 1) * 64] for i in range(NZ)], axis=1))
        return jnp.concatenate(out, axis=0).astype(BF16)

    loads[0].wait()
    keep(FIELD, columns_of(field_ref))
    loads[1].wait()
    keep(COT, columns_of(cot_ref))
    pl.semaphore_wait(barrier, len(sides) + 2 * (ring - 1) + 2 * n_x - 1)
    for d in range(8):
        halo(FIELD, d).start()
    for d in range(8):
        halo(COT, d).start()

    def build_band(layer, ref):
        nothing = jnp.zeros((64, 64), F32)
        for k in range(9):
            low, mid, high = (
                ref[:, (3 * k + i) * 64 : (3 * k + i + 1) * 64].astype(F32) for i in range(3)
            )
            lanes = slice((k % 3) * WIDE, (k % 3 + 1) * WIDE)
            for out_z, parts in enumerate(
                (
                    (mid, high, nothing, nothing),
                    (low, mid, high, nothing),
                    (nothing, low, mid, high),
                    (nothing, nothing, low, mid),
                )
            ):
                band[layer, k // 3, out_z * 64 : (out_z + 1) * 64, lanes] = jnp.concatenate(
                    parts, axis=1
                ).astype(BF16)

    loads[2].wait()
    build_band(0, first_ref)
    loads[3].wait()
    build_band(1, second_ref)
    loads[4].wait()
    framed_rows = (TX + 2) * TY
    source_rows = (TX + 8) * TY
    i = iota((framed_rows, 1), 0)
    r = lax.div(i, TY)
    c = lax.rem(i, TY)
    first_row, last_row = jnp.where(gx == 0, 0, -1), jnp.where(gx == n_gx - 1, TX + 1, -1)
    first_col, last_col = jnp.where(gy == 0, 0, -1), jnp.where(gy == n_gy - 1, TY - 1, -1)
    outside = (r == first_row) | (r == last_row)

    def shifted(step, at, column_slot, low_slot, high_slot, pick, outer):
        edge = jnp.where(
            r == 0,
            low_slot * TY + pick,
            jnp.where(r == TX + 1, high_slot * TY + pick, column_slot * TY + r - 1),
        )
        target = jnp.where(c == at, edge, i + step)
        return onehot(jnp.where(outside | (c == outer), -1, target), (framed_rows, source_rows))

    shift_low = shifted(-1, 0, TX + 2, TX + 4, TX + 6, TY - 1, first_col)
    shift_high = shifted(1, TY - 1, TX + 3, TX + 5, TX + 7, 0, last_col)
    above = jnp.where(gx == 0, 0.0, 1.0)
    below = jnp.where(gx == n_gx - 1, 0.0, 1.0)

    def frame(a):
        for d in range(8):
            halo(a, d).wait_recv()
        whole = src[a].reshape(source_rows, WIDE)
        cat[a, :, 0:WIDE] = dot(shift_low, whole).astype(BF16)
        cat[a, :, 2 * WIDE : 3 * WIDE] = dot(shift_high, whole).astype(BF16)
        cat[a, 0:TY, WIDE : 2 * WIDE] = (src[a, 0].astype(F32) * above).astype(BF16)
        cat[a, TY : TY + CELLS, WIDE : 2 * WIDE] = src[a, 1 : TX + 1].reshape(CELLS, WIDE)
        cat[a, TY + CELLS :, WIDE : 2 * WIDE] = (src[a, TX + 1].astype(F32) * below).astype(BF16)

    def rows_of(a, dx):
        return cat[a, dx * TY : dx * TY + CELLS, :]

    def convolve(a, layer):
        return sum(dot(rows_of(a, dx), band[layer, dx], NT) for dx in range(3))

    sample = samples_ref[...]
    sample_cell = jnp.broadcast_to(lax.div(sample, NZ).astype(F32), (256, 256)).T
    sample_level = jnp.broadcast_to(lax.rem(sample, NZ).astype(F32), (256, 256)).T
    lane = iota((256, 256), 1)
    gather = jnp.where(sample_cell == lane.astype(F32), 1.0, 0.0).astype(BF16)
    level = jnp.where(sample_level == lax.div(lane, C).astype(F32), 1.0, 0.0)
    low_lanes = iota((64, 128), 1) < 64

    def gram(values):
        picked = dot(gather, values) * level
        full_gram = dot(picked.T.astype(BF16), picked.astype(BF16))
        even = full_gram[0:64, 0:128] + full_gram[128:192, 128:256]
        odd = full_gram[64:128, 0:128] + full_gram[192:256, 128:256]
        return even, odd

    count = float(n_gx * n_gy * 256)
    scale = 1.0 / jnp.sqrt(jnp.float32(n_gx * n_gy * CELLS * NZ))

    def two_grams(one, two):
        even, odd = gram(one)
        even2, odd2 = gram(two)
        both = jnp.where(low_lanes, even + swap_halves(odd), swap_halves(even2) + odd2)
        return (both / count).reshape(ring // 2, 128 // ring, 128)

    field = src[FIELD, 1 : TX + 1].reshape(CELLS, WIDE)
    cot = src[COT, 1 : TX + 1].reshape(CELLS, WIDE)
    gram_pay[: ring // 2] = two_grams(field, cot)

    chunk = HALF // ring

    def assemble(layer, flip):
        taps = [None] * 27
        for dx in range(3):
            for dy in range(3):

                def piece(a, h):
                    at = dy * WIDE + h * 128
                    return grads[layer, dx, a * 64 : (a + 1) * 64, at : at + 128]

                even, odd = piece(0, 0) + piece(2, 1), piece(1, 0) + piece(3, 1)
                pairs = ((odd, piece(2, 0)), (even, odd), (piece(1, 1), even))
                for e in range(3):
                    tap = (dx * 3 + dy) * 3 + e
                    taps[26 - tap if flip else tap] = pairs[e]
        for k in range(BLOCKS // 2):
            low, high = 2 * k, 2 * k + 1
            value = jnp.zeros((64, 128), F32)
            if low < 27:
                value = jnp.where(low_lanes, taps[low][0] + swap_halves(taps[low][1]), 0.0) * scale
            if high < 27:
                other = (swap_halves(taps[high][0]) + taps[high][1]) * scale
                value = jnp.where(low_lanes, value, other)
            per = chunk // 128
            half, rest = divmod(k, ring * per)
            at, p = divmod(rest, per)
            pay[layer, half, at, p * 64 : (p + 1) * 64, :] = value

    def send_on(layer):
        for k in ones[layer].order:
            from_core(layer, k).wait_recv()
            j = lax.rem(rank + k, ring)
            pay[layer, core, j] = pay[layer, core, j] + core_in[layer, j]
            ones[layer].outgoing(k).start()
        from_core(layer, 0).wait_recv()
        one_in[layer, rank] = pay[layer, core, rank] + core_in[layer, rank]

    frame(FIELD)
    hidden_pre = convolve(FIELD, 0)
    sigma = 1.0 / (1.0 + jnp.exp(-hidden_pre))
    hidden = (hidden_pre * sigma).astype(BF16)
    keep(HIDDEN, hidden)
    for d in range(8):
        halo(HIDDEN, d).start()

    frame(COT)
    hidden_t = hidden.astype(F32).T.astype(BF16)
    for dx in range(3):
        grads[1, dx] = dot(hidden_t, rows_of(COT, dx))
    assemble(1, True)
    for k in ones[1].order + [0]:
        to_core(1, k).start()

    back = jnp.zeros((CELLS, WIDE), F32)
    for dx in range(3):
        for dy in range(3):
            back += dot(
                cat[COT, dx * TY : dx * TY + CELLS, dy * WIDE : (dy + 1) * WIDE],
                band[1, 2 - dx, :, (2 - dy) * WIDE : (3 - dy) * WIDE],
            )
    delta = (back * sigma * (1.0 + hidden_pre * (1.0 - sigma))).astype(BF16)
    gram_pay[ring // 2 :] = two_grams(hidden, delta)
    gram_first.start()
    gram_one[y] = gram_pay[y]
    send_on(1)

    delta_t = delta.astype(F32).T.astype(BF16)
    for dx in range(3):
        grads[0, dx] = dot(delta_t, rows_of(FIELD, dx))
    assemble(0, False)
    for k in ones[0].order + [0]:
        to_core(0, k).start()
    send_on(0)

    gram_first.wait()
    gram_two[z] = jnp.sum(gram_one[...], axis=0)
    gram_second.start()

    frame(HIDDEN)
    output = (field.astype(F32) + convolve(HIDDEN, 1)).astype(BF16).astype(F32)
    for b in range(4):
        block = output[b * 64 : (b + 1) * 64]
        stacked = jnp.concatenate([block[:, j * 64 : (j + 1) * 64] for j in range(NZ)], axis=0)
        out_ref[b * 256 : (b + 1) * 256, :] = dot(to_cells, stacked.astype(BF16)).astype(BF16)
    store_out = pltpu.make_async_copy(out_ref, out_hbm, store_sem.at[0])
    store_out.start()

    part = chunk // 2 // ring
    for layer in range(2):
        ones[layer].wait()
        total = one_in[layer, 0]
        for j in range(1, ring):
            total += one_in[layer, j]
        two_out[:, layer * part : (layer + 1) * part] = total.reshape(ring, part, 128)
    two_in[rank_two] = two_out[rank_two]
    two.start()
    for a in range(3):
        for d in range(8):
            halo(a, d).wait_send()

    gram_second.wait()
    gram_x[seat] = jnp.sum(gram_two[...], axis=0)
    gram_third.start()

    gram_third.wait()
    gram_all[y] = jnp.sum(gram_x[...], axis=0)
    gram_gather.start()
    for k in range(ring):
        to_core(1, k).wait_send()
        to_core(0, k).wait_send()

    two.wait()
    x_in[x] = jnp.sum(two_in[...], axis=0)
    third.start()
    for stage in (ones[1], ones[0], gram_first):
        stage.settle()
    third.wait()
    whole[rank_two] = jnp.sum(x_in[...], axis=0)
    gather_two.start()

    gram_gather.wait()

    grams = gram_all[...].reshape(2, 64, 128)
    metric[...] = jnp.zeros((256, 256), F32)
    for m in range(4):
        lanes = slice((m // 2) * 128, (m // 2 + 1) * 128)
        mine = low_lanes if m % 2 == 0 else jnp.logical_not(low_lanes)
        block = grams[m // 2]
        metric[m * 64 : (m + 1) * 64, lanes] = jnp.where(mine, block, 0.0)
    eye = jnp.where(iota((256, 256), 0) == lane, 1.0, 0.0)
    matrix = metric[...] + 0.1 * eye
    norms = [
        jnp.sqrt(jnp.sum(matrix[m * 64 : (m + 1) * 64] * matrix[m * 64 : (m + 1) * 64]))
        for m in range(4)
    ]
    error = eye - jnp.concatenate(
        [matrix[m * 64 : (m + 1) * 64] / norms[m] for m in range(4)], axis=0
    )
    factor = eye + error
    parts = split(error)
    error = dot3(parts, parts)
    for step in range(1, NS_ITERS):
        parts = split(error)
        if step < NS_ITERS - 1:
            both = tuple(jnp.concatenate([f, e], axis=0) for f, e in zip(split(factor), parts))
            moved = dot3(both, parts)
            factor, error = factor + moved[0:256], moved[256:512]
        else:
            factor = factor + dot3(split(factor), parts)
    approx = jnp.concatenate([factor[m * 64 : (m + 1) * 64] / norms[m] for m in range(4)], axis=0)

    def twice(block, low):
        other = swap_halves(block)
        first, second = (block, other) if low else (other, block)
        return split(
            jnp.concatenate(
                [jnp.where(low_lanes, first, 0.0), jnp.where(low_lanes, 0.0, second)], axis=0
            )
        )

    left_first = twice(approx[0:64, 0:128], True)
    right_second = twice(approx[64:128, 0:128], False)
    none = jnp.zeros((64, 128), F32)
    left_second = split(
        jnp.concatenate([jnp.where(low_lanes, approx[128:192, 128:256], 0.0), none], axis=0)
    )
    right_first = split(
        jnp.where(low_lanes, swap_halves(approx[192:256, 128:256]), 0.0)
    )

    for stage in (two, third, gram_second, gram_third, gram_gather):
        stage.settle()
    gather_two.wait()
    pairs = chunk // 128
    both = [
        whole[:, layer * part : (layer + 1) * part].reshape(pairs, 64, 128) for layer in range(2)
    ]
    for p in range(pairs):
        block = split(jnp.concatenate([both[0][p], none], axis=0))
        result[core, rank, p, 0:64, :] = dot3(
            right_first, split(dot3(block, left_first))
        ).astype(BF16)
        block = split(jnp.concatenate([both[1][p], none], axis=0))
        done = dot3(split(dot3_t(right_second, block)), left_second)
        result[core, rank, p, 64:128, :] = jnp.where(
            low_lanes, done[0:64], swap_halves(done[64:128])
        ).astype(BF16)
    spread.start()
    gather_two.settle()
    to_back(0).start()
    for k in reversed(spread.order):
        spread.arrived(k)
        to_back(k).start()
    spread.settle()
    for k in [0] + spread.order[::-1]:
        from_back(k).wait_recv()

    for k in range(14):
        half, rest = divmod(k, HALF // 128)
        at, p = divmod(rest, pairs)
        lanes = 128 if k < 13 else 64
        first_out[:, k * 128 : k * 128 + lanes] = result[half, at, p, 0:64, 0:lanes]
        second_out[:, k * 128 : k * 128 + lanes] = result[half, at, p, 64:128, 0:lanes]

    for k in range(ring):
        to_back(k).wait_send()
    store_out.wait()


def solution(mesh):
    n_gx, n_gy = mesh.shape["gx"], mesh.shape["gy"]
    ring = n_gx // 4
    z_hi = ring // 2
    n_x = n_gy // z_hi
    chunk = HALF // ring
    most = max(ring, 2 * n_x)
    vmem = pl.BlockSpec(memory_space=pltpu.VMEM)
    anywhere = pl.BlockSpec(memory_space=pl.ANY)
    dma = pltpu.SemaphoreType.DMA

    def local(field, first_kernel, second_kernel, cotangent, samples):
        cells = field.shape[0] * field.shape[1] * field.shape[2]
        output, first, second = pl.pallas_call(
            functools.partial(kernel, (n_gx, n_gy, z_hi, ring, n_x)),
            out_shape=(
                jax.ShapeDtypeStruct((cells, C), BF16),
                jax.ShapeDtypeStruct((C, 27 * C), BF16),
                jax.ShapeDtypeStruct((C, 27 * C), BF16),
            ),
            in_specs=[anywhere] * 5,
            out_specs=(anywhere, vmem, vmem),
            scratch_shapes=[
                pltpu.VMEM((cells, C), BF16),
                pltpu.VMEM((C, 27 * C), BF16),
                pltpu.VMEM((C, 27 * C), BF16),
                pltpu.VMEM((cells, C), BF16),
                pltpu.VMEM((1, 256), jnp.int32),
                pltpu.VMEM((cells, C), BF16),
                pltpu.VMEM((3, TX + 8, TY, WIDE), BF16),
                pltpu.VMEM((3, 2, TX, WIDE), BF16),
                pltpu.VMEM((3, (TX + 2) * TY, 3 * WIDE), BF16),
                pltpu.VMEM((2, 3, WIDE, 3 * WIDE), BF16),
                pltpu.VMEM((2, 3, WIDE, 3 * WIDE), F32),
                pltpu.VMEM((2, 2, ring, chunk // 2, 128), F32),
                pltpu.VMEM((2, ring, chunk // 2, 128), F32),
                pltpu.VMEM((2, ring, chunk // 2, 128), F32),
                pltpu.VMEM((ring, chunk // ring, 128), F32),
                pltpu.VMEM((ring, chunk // ring, 128), F32),
                pltpu.VMEM((n_x, chunk // ring, 128), F32),
                pltpu.VMEM((ring, chunk // ring, 128), F32),
                pltpu.VMEM((2, ring, chunk // 128, 128, 128), BF16),
                pltpu.VMEM((ring, 128 // ring, 128), F32),
                pltpu.VMEM((ring, 128 // ring, 128), F32),
                pltpu.VMEM((ring, 128 // ring, 128), F32),
                pltpu.VMEM((2 * n_x, 128 // ring, 128), F32),
                pltpu.VMEM((ring, 128 // ring, 128), F32),
                pltpu.VMEM((256, 256), F32),
                dma((5,)),
                dma((1,)),
                dma((3, 8)),
                dma((3, 8)),
                dma((14, most)),
                dma((14, most)),
            ],
            compiler_params=pltpu.CompilerParams(
                collective_id=0, has_side_effects=True, vmem_limit_bytes=(53 * 1024 + 360) * 1024
            ),
        )(
            field.reshape(cells, C),
            first_kernel.T,
            second_kernel.T,
            cotangent.reshape(cells, C),
            samples.reshape(1, -1),
        )
        return output.reshape(field.shape), first.astype(F32).T, second.astype(F32).T

    placed = (P("gx", "gy", None, None), P(), P(), P("gx", "gy", None, None), P("gx", "gy", None))
    return jax.shard_map(
        local,
        mesh=mesh,
        in_specs=placed,
        out_specs=(P("gx", "gy", None, None), P(), P()),
        check_vma=False,
    )
```
